32 devices in a mesh: seq: 8 (over z, x), fsdp: 4 (over y, core).
Axes of the slice: x: 2, y: 2, z: 4, core: 2. Of those that a mesh axis runs over, the one named last changes fastest.
Arguments:
- residual_in: float32 [4, 4096, 1024], P('fsdp', 'seq'), may hold values from -16 to 16, as said below
- doc_starts: int32 [4, 4096], P('fsdp', 'seq'), may hold values from 0 to 1, as said below
- out_grad: float32 [4, 4096, 1024], P('fsdp', 'seq'), may hold values from -6 to 6
- norm_gain: float32 [1024], P('fsdp'), may hold values from 0.5 to 1.5
- qkv_weight: float32 [1024, 4096], P('fsdp'), may hold values from -0.1875 to 0.1875
- gate_weight: float32 [1024, 2048], P('fsdp'), may hold values from -0.1875 to 0.1875
- decay_beta_weight: float32 [1024, 16], P('fsdp'), may hold values from -0.1875 to 0.1875
- conv_weight: float32 [4, 4096], P(None, 'fsdp'), may hold values from -3 to 3
- decay_log: float32 [8], P('fsdp'), as said below
- decay_bias: float32 [8], P('fsdp'), may hold values from -1 to 1
- beta_bias: float32 [8], P('fsdp'), as said below
- head_gain: float32 [256], P('fsdp'), may hold values from 0.5 to 1.5
- out_weight: float32 [2048, 1024], P('fsdp'), may hold values from -0.125 to 0.125
- mlp_gain: float32 [1024], P('fsdp'), may hold values from 0.5 to 1.5
- up_weight: float32 [1024, 5632], P('fsdp'), may hold values from -0.1875 to 0.1875
- down_weight: float32 [2816, 1024], P('fsdp'), may hold values from -0.109375 to 0.109375
Outputs:
- output: float32 [4, 4096, 1024], P('fsdp', 'seq')
- input_grad: float32 [4, 4096, 1024], P('fsdp', 'seq')
- grad_norm_gain: float32 [1024], P('fsdp')
- grad_qkv_weight: float32 [1024, 4096], P('fsdp')
- grad_gate_weight: float32 [1024, 2048], P('fsdp')
- grad_decay_beta_weight: float32 [1024, 16], P('fsdp')
- grad_conv_weight: float32 [4, 4096], P(None, 'fsdp')
- grad_decay_log: float32 [8], P('fsdp')
- grad_decay_bias: float32 [8], P('fsdp')
- grad_beta_bias: float32 [8], P('fsdp')
- grad_head_gain: float32 [256], P('fsdp')
- grad_out_weight: float32 [2048, 1024], P('fsdp')
- grad_mlp_gain: float32 [1024], P('fsdp')
- grad_up_weight: float32 [1024, 5632], P('fsdp')
- grad_down_weight: float32 [2816, 1024], P('fsdp')
- rms: float32 [4], replicated
The draws below stay inside these ranges and needn't reach their ends.
Inputs may be any that keep to these rules, and one draw needn't show every extreme that they name: `doc_starts`: 1 where a document starts, else 0; the first token of each sequence starts a document; in each sequence one document starts within its first 256 tokens and runs until a start within its last 256 tokens. `residual_in`: rows whose scale changes along the sequence. `decay_log`: the log of a per-token rate between 0.3 / 4096 and 1 / 30. `beta_bias`: a logit between that of 16 / 4096 and 1.5.
All inputs are finite; a program needn't handle non-finite values.
Results may differ from the reference program's by a relative error of at most 0.0003.
Values sent between devices are 32-bit elements; how exact they have to be, the bound alone decides.
No kernel may reach another device: no remote copies, remote signals or barrier semaphores. Data moves between devices by JAX's collectives and lax.ppermute only.
A program may use at most 640 MiB of HBM per device.

```python
import math
import jax
import jax.numpy as jnp
from jax import lax

D = 1024
H = 8
DK = 128
DV = 256
FF = 2816
CONV = 4
BLOCK = 64
TOK_DEV = 512
LENGTH = 4096
SEQS = 4


def slow_heads(key, count):
    order = jax.random.permutation(key, H)
    return order < count


def draw_decay_log(key, part):
    slow = slow_heads(key, H // 2)
    key = jax.random.fold_in(key, 11)
    first, second = jax.random.split(key)
    slow_rate = jnp.exp(jax.random.uniform(first, (H,), jnp.float32, math.log(0.3), math.log(2.0))) / LENGTH
    fast_rate = 1.0 / jax.random.uniform(second, (H,), jnp.float32, 30.0, 50.0)
    return jnp.log(jnp.where(slow, slow_rate, fast_rate))


def draw_beta_bias(key, part):
    slow = slow_heads(key, H // 2)
    key = jax.random.fold_in(key, 13)
    first, second = jax.random.split(key)
    slow_beta = 32.0 / LENGTH * jnp.exp(jax.random.uniform(first, (H,), jnp.float32, math.log(0.5), math.log(2.0)))
    fast_bias = jax.random.uniform(second, (H,), jnp.float32, -0.5, 1.5)
    return jnp.where(slow, jnp.log(slow_beta / (1.0 - slow_beta)), fast_bias)


def draw_residual_in(key, part):
    key = jax.random.fold_in(key, 17)
    position = jnp.arange(LENGTH, dtype=jnp.float32) / (LENGTH - 1)
    base = jax.random.truncated_normal(key, -5.0, 5.0, (SEQS, LENGTH, D), jnp.float32)
    scale = 1.0 + 2.0 * position
    return base * scale[None, :, None]


def draw_doc_starts(key, part):
    key = jax.random.fold_in(key, 19)
    first, second, third = jax.random.split(key, 3)
    half = max(TOK_DEV // 2, 2)
    begin = jax.random.randint(first, (SEQS, 1), 1, half)
    ending = LENGTH - jax.random.randint(second, (SEQS, 1), 1, half)
    position = jnp.arange(LENGTH)[None, :]
    extra = jax.random.randint(third, (SEQS, LENGTH), 0, 24) == 0
    outside = (position < begin) | (position > ending)
    flags = (position == 0) | (position == begin) | (position == ending) | extra & outside
    return flags.astype(jnp.int32)


def shard_levels(stream_key, shape, cuts, smallest, high):
    loudness = 1.0
    for dim, shards_of in cuts:
        heights = jax.random.uniform(jax.random.fold_in(jax.random.fold_in(stream_key, 6), dim), (shards_of,), jnp.float32, smallest / len(cuts), high / len(cuts))
        loudness = loudness * jnp.repeat(jnp.exp(heights), shape[dim] // shards_of).reshape((-1,) + (1,) * (len(shape) - 1 - dim))
    return loudness


def scatter_about(own_key, shape, scale, bound, shards=(), held_as=jnp.bfloat16):
    drawn = jax.random.normal(own_key, shape, jnp.float32) * scale
    if len(shards) > 0:
        drawn = shard_levels(own_key, shape, shards, -0.22, 0.18) * drawn
    return jnp.clip(drawn, min=-bound, max=bound).astype(held_as)


def setup_inputs(seed: int = 0) -> dict:
    arg_keys = jax.random.split(jax.random.key(seed), 17)
    residual_in = draw_residual_in(jax.random.fold_in(arg_keys[16], 71), 0)
    doc_starts = draw_doc_starts(jax.random.fold_in(arg_keys[16], 71), 0)
    out_grad = scatter_about(arg_keys[2], (SEQS, LENGTH, D), 1.0, 6.0, ((0, 4), (1, 8)), jnp.float32)
    norm_gain = jnp.clip(1.0 + 0.1 * jax.random.normal(arg_keys[3], (D,), jnp.float32), 0.5, 1.5)
    qkv_weight = scatter_about(arg_keys[4], (D, 2 * H * DK + H * DV), D ** -0.5, 0.1875, ((0, 4),), jnp.float32)
    gate_weight = scatter_about(arg_keys[5], (D, H * DV), D ** -0.5, 0.1875, ((0, 4),), jnp.float32)
    decay_beta_weight = scatter_about(arg_keys[6], (D, 2 * H), D ** -0.5, 0.1875, ((0, 4),), jnp.float32)
    conv_weight = scatter_about(arg_keys[7], (CONV, 2 * H * DK + H * DV), CONV ** -0.5, 3.0, ((1, 4),), jnp.float32)
    decay_log = draw_decay_log(jax.random.fold_in(arg_keys[16], 71), 0)
    decay_bias = jnp.clip(jax.random.uniform(arg_keys[9], (H,), jnp.float32, -1.0, 1.0) * shard_levels(arg_keys[9], (H,), ((0, 4),), -0.4, 0.0), -1.0, 1.0)
    beta_bias = draw_beta_bias(jax.random.fold_in(arg_keys[16], 71), 0)
    head_gain = jnp.clip(1.0 + 0.1 * jax.random.normal(arg_keys[11], (DV,), jnp.float32), 0.5, 1.5)
    out_weight = scatter_about(arg_keys[12], (H * DV, D), (H * DV) ** -0.5, 0.125, ((0, 4),), jnp.float32)
    mlp_gain = jnp.clip(1.0 + 0.1 * jax.random.normal(arg_keys[13], (D,), jnp.float32), 0.5, 1.5)
    up_weight = scatter_about(arg_keys[14], (D, 2 * FF), D ** -0.5, 0.1875, ((0, 4),), jnp.float32)
    down_weight = scatter_about(arg_keys[15], (FF, D), FF ** -0.5, 0.109375, ((0, 4),), jnp.float32)
    return {"residual_in": residual_in, "doc_starts": doc_starts, "out_grad": out_grad, "norm_gain": norm_gain, "qkv_weight": qkv_weight, "gate_weight": gate_weight, "decay_beta_weight": decay_beta_weight, "conv_weight": conv_weight, "decay_log": decay_log, "decay_bias": decay_bias, "beta_bias": beta_bias, "head_gain": head_gain, "out_weight": out_weight, "mlp_gain": mlp_gain, "up_weight": up_weight, "down_weight": down_weight}


HIGH_PRECISION = lax.Precision.HIGHEST
NORM_EPS = 1e-05
UNIT_EPS = 1e-06

def matmul(left, right):
    return jnp.dot(left, right, precision=HIGH_PRECISION, preferred_element_type=jnp.float32)

def rms_norm(rows, gain):
    return rows * lax.rsqrt(lax.optimization_barrier(jnp.mean(rows * rows, axis=-1, keepdims=True)) + NORM_EPS) * gain

def unit_rows(rows):
    return rows * lax.rsqrt(lax.optimization_barrier(jnp.sum(rows * rows, axis=-1, keepdims=True)) + UNIT_EPS)

def delta_rule(queries, key_rows, values, decays, beta_rows):
    length = queries.shape[0]

    def token_step(carried_state, pieces):
        single_query, single_key, one_value, one_decay, one_beta = pieces
        carried_state = one_decay[:, None, None] * carried_state
        recalled_values = jnp.einsum('dgl,dg->dl', carried_state, single_key, precision=HIGH_PRECISION)
        update = (one_beta[:, None] * (one_value - recalled_values))[:, None, :] * single_key[:, :, None]
        carried_state = carried_state + update
        return (carried_state, jnp.einsum('dgl,dg->dl', carried_state, single_query, precision=HIGH_PRECISION))

    def block_step(carried_state, pieces):
        return lax.scan(token_step, carried_state, pieces)
    shaped = tuple((piece.reshape((length // BLOCK, BLOCK) + piece.shape[1:]) for piece in (queries, key_rows, values, decays, beta_rows)))
    start_state = jnp.zeros((H, DK, DV), jnp.float32)
    final_state, outputs = lax.scan(jax.checkpoint(block_step), start_state, shaped)
    return outputs.reshape(length, H, DV)

def finish(head_outputs, gate_rows, rows, head_gain, out_weight, mlp_gain, up_weight, down_weight):
    length = rows.shape[0]
    scaled = head_outputs * lax.rsqrt(lax.optimization_barrier(jnp.mean(head_outputs * head_outputs, axis=-1, keepdims=True)) + NORM_EPS)
    gated = scaled * head_gain * jax.nn.silu(gate_rows.reshape(length, H, DV))
    mixer = matmul(gated.reshape(length, H * DV), out_weight)
    middle = rows + mixer
    lifted = matmul(rms_norm(middle, mlp_gain), up_weight)
    hidden = jax.nn.silu(lifted[:, :FF]) * lifted[:, FF:]
    branch = matmul(hidden, down_weight)
    return (middle + branch, mixer, branch)

def block(rows, starts, weights):
    norm_gain, qkv_weight, gate_weight, decay_beta_weight, conv_weight, decay_log, decay_bias, beta_bias, head_gain, out_weight, mlp_gain, up_weight, down_weight = weights
    length = rows.shape[0]
    normed = rms_norm(rows, norm_gain)
    mixed_in = matmul(normed, qkv_weight)
    gate_rows = matmul(normed, gate_weight)
    decay_beta = matmul(normed, decay_beta_weight)
    counts = jnp.cumsum(starts).astype(jnp.int32)
    convolved = conv_weight[0] * mixed_in
    for shift_by in range(1, CONV):
        earlier = jnp.concatenate([jnp.zeros((shift_by, mixed_in.shape[1]), jnp.float32), mixed_in[:-shift_by]], 0)
        earlier_counts = jnp.concatenate([jnp.full((shift_by,), -1, jnp.int32), counts[:-shift_by]], 0)
        same = (counts == earlier_counts).astype(jnp.float32)
        convolved = convolved + conv_weight[shift_by] * earlier * same[:, None]
    convolved = jax.nn.silu(convolved)
    width_k = H * DK
    queries = unit_rows(convolved[:, :width_k].reshape(length, H, DK)) * DK ** (-0.5)
    key_rows = unit_rows(convolved[:, width_k:2 * width_k].reshape(length, H, DK))
    values = convolved[:, 2 * width_k:].reshape(length, H, DV)
    log_decay = -jnp.exp(decay_log) * jax.nn.softplus(decay_beta[:, :H] + decay_bias)
    beta_rows = jax.nn.sigmoid(decay_beta[:, H:] + beta_bias)
    decays = jnp.exp(log_decay) * (1 - starts).astype(jnp.float32)[:, None]
    head_outputs = delta_rule(queries, key_rows, values, decays, beta_rows)
    result, mixer, branch = finish(head_outputs, gate_rows, rows, head_gain, out_weight, mlp_gain, up_weight, down_weight)
    squares = jnp.stack([jnp.sum(rows * rows), jnp.sum(mixer * mixer), jnp.sum(branch * branch), jnp.sum(result * result)])
    return (result, squares)

def add_pair(first, second):
    return first + second

def reference(residual_in, doc_starts, out_grad, norm_gain, qkv_weight, gate_weight, decay_beta_weight, conv_weight, decay_log, decay_bias, beta_bias, head_gain, out_weight, mlp_gain, up_weight, down_weight):
    weights = (norm_gain, qkv_weight, gate_weight, decay_beta_weight, conv_weight, decay_log, decay_bias, beta_bias, head_gain, out_weight, mlp_gain, up_weight, down_weight)
    outputs = []
    input_grads = []
    totals = jax.tree.map(jnp.zeros_like, weights)
    squares = jnp.zeros((4,), jnp.float32)
    for seq_index in range(SEQS):
        starts = doc_starts[seq_index]

        def run(rows, params):
            return block(rows, starts, params)
        result, pull, extras = jax.vjp(run, residual_in[seq_index], weights, has_aux=True)
        row_grad, weight_grads = pull(out_grad[seq_index])
        outputs.append(result)
        input_grads.append(row_grad)
        totals = jax.tree.map(add_pair, totals, weight_grads)
        squares = squares + extras
    rms = jnp.sqrt(squares / (SEQS * LENGTH * D))
    return (jnp.stack(outputs), jnp.stack(input_grads), totals[0], totals[1], totals[2], totals[3], totals[4], totals[5], totals[6], totals[7], totals[8], totals[9], totals[10], totals[11], totals[12], rms)
```

```python
from functools import partial

import jax
import jax.numpy as jnp
from jax import lax
from jax.experimental import pallas as pl
from jax.experimental.pallas import tpu as pltpu
from jax.sharding import PartitionSpec as P

D = 1024
H = 8
DK = 128
DV = 256
FF = 2816
CONV = 4
C = 64

NORM_EPS = 1e-05
UNIT_EPS = 1e-06
F32 = jnp.float32
BF16 = jnp.bfloat16
VMEM_BYTES = 48 * 1024 * 1024

NN = (((1,), (0,)), ((), ()))
NT = (((1,), (1,)), ((), ()))
TN = (((0,), (0,)), ((), ()))


def swapped(block, axis, distance):
    return lax.ppermute(block, axis, [(i, i ^ distance) for i in range(lax.axis_size(axis))])


def passed_along(block, axis, distance):
    devices = range(lax.axis_size(axis))
    route = [(i - distance, i) for i in devices if i - distance in devices]
    return lax.ppermute(block, axis, route)


def rows_of(block, start, size):
    return lax.dynamic_slice_in_dim(block, start, size, 0)


def columns_of(block, start, size):
    return lax.dynamic_slice_in_dim(block, start, size, 1)


def gathered_weight(shard, bit):
    half = shard.shape[0] // 2
    near = swapped(shard, "fsdp", 1)
    far_a = swapped(rows_of(shard, bit * half, half), "fsdp", 2)
    far_b = swapped(far_a, "seq", 1)
    return [
        shard,
        near,
        far_a,
        far_b,
        swapped(far_a, "fsdp", 1),
        swapped(far_b, "fsdp", 1),
    ]


def block_starts(shard_rows, place, bit):
    half = shard_rows // 2
    far, last = (place ^ 2) * shard_rows, (place ^ 3) * shard_rows
    return [
        (place * shard_rows, shard_rows),
        ((place ^ 1) * shard_rows, shard_rows),
        (far + bit * half, half),
        (far + (1 - bit) * half, half),
        (last + bit * half, half),
        (last + (1 - bit) * half, half),
    ]


def reduced_shard(grads, bits):
    first = grads[0] + swapped(grads[1], "fsdp", 1)
    second = grads[2] + swapped(grads[3], "fsdp", 1)
    total = first + swapped(second, "fsdp", 2)
    for step, bit in enumerate(bits):
        half = total.shape[0] // 2
        kept = rows_of(total, bit * half, half)
        total = kept + swapped(rows_of(total, (1 - bit) * half, half), "seq", 1 << step)
    for step, bit in reversed(list(enumerate(bits))):
        half = total.shape[0]
        other = swapped(total, "seq", 1 << step)
        whole = jnp.zeros((2 * half, total.shape[1]), F32)
        whole = lax.dynamic_update_slice_in_dim(whole, total, bit * half, 0)
        total = lax.dynamic_update_slice_in_dim(whole, other, (1 - bit) * half, 0)
    return total


def summed_small(rows4, bits):
    near = swapped(rows4[1::2], "fsdp", 1)
    pair = rows4[0::2] + near
    total = pair[0] + swapped(pair[1], "fsdp", 2)
    for step in range(len(bits)):
        total = total + swapped(total, "seq", 1 << step)
    return total


def dot(left, right, dims=NN):
    return lax.dot_general(
        left, right, dims, precision=lax.Precision.HIGH, preferred_element_type=F32
    )


def split(x):
    high = x.astype(BF16)
    return high, (x - high.astype(F32)).astype(BF16)


def dot3(left, right, dims=NN):
    lh, ll = split(left)
    rh, rl = split(right)
    one = partial(lax.dot_general, dimension_numbers=dims, preferred_element_type=F32)
    return one(lh, rh) + (one(lh, rl) + one(ll, rh))


def rms_norm(rows, gain):
    return rows * lax.rsqrt(jnp.mean(rows * rows, axis=-1, keepdims=True) + NORM_EPS) * gain


def unit_rows(rows):
    return rows * lax.rsqrt(jnp.sum(rows * rows, axis=-1, keepdims=True) + UNIT_EPS)


def front(mixed_in, rim_rows, decay_beta, conv_weight, decay_log, decay_bias, beta_bias, counts):
    tokens_here = mixed_in.shape[0]
    extended = jnp.concatenate([rim_rows, mixed_in], 0)
    extended_counts = jnp.concatenate([jnp.zeros((CONV - 1,), jnp.int32), counts], 0)
    convolved = conv_weight[0] * mixed_in
    for shift_by in range(1, CONV):
        offset = CONV - 1 - shift_by
        same = (counts == extended_counts[offset : offset + tokens_here]).astype(F32)
        convolved = (
            convolved
            + conv_weight[shift_by] * extended[offset : offset + tokens_here] * same[:, None]
        )
    convolved = jax.nn.silu(convolved)
    width_k = H * DK
    queries = unit_rows(convolved[:, :width_k].reshape(tokens_here, H, DK)) * DK ** (-0.5)
    key_rows = unit_rows(convolved[:, width_k : 2 * width_k].reshape(tokens_here, H, DK))
    values = convolved[:, 2 * width_k :]
    log_decay = -jnp.exp(decay_log) * jax.nn.softplus(decay_beta[:, :H] + decay_bias)
    beta_rows = jax.nn.sigmoid(decay_beta[:, H:] + beta_bias)
    return (
        queries.reshape(tokens_here, width_k),
        key_rows.reshape(tokens_here, width_k),
        values,
        log_decay,
        beta_rows,
    )


def gate_heads(head_outputs, gate_rows, head_gain):
    tokens_here = head_outputs.shape[0]
    heads = head_outputs.reshape(tokens_here, H, DV)
    scaled = heads * lax.rsqrt(jnp.mean(heads * heads, axis=-1, keepdims=True) + NORM_EPS)
    gated = scaled * head_gain * jax.nn.silu(gate_rows.reshape(tokens_here, H, DV))
    return gated.reshape(tokens_here, H * DV)


def swiglu(lifted):
    return jax.nn.silu(lifted[:, :FF]) * lifted[:, FF:]


def call(kernel, grid, in_specs, out_specs, out_shapes, scratch=(), name=None, flops=0, bytes_=0):
    return pl.pallas_call(
        kernel,
        grid=grid,
        in_specs=in_specs,
        out_specs=out_specs,
        out_shape=out_shapes,
        scratch_shapes=scratch,
        name=name,
        compiler_params=pltpu.CompilerParams(
            vmem_limit_bytes=VMEM_BYTES,
            dimension_semantics=("arbitrary",) * len(grid),
        ),
        cost_estimate=pl.CostEstimate(flops=flops, bytes_accessed=bytes_, transcendentals=0),
    )


def shape(*dims):
    return jax.ShapeDtypeStruct(dims, F32)


def head_block(tokens, width):
    return pl.BlockSpec((tokens, width), lambda h: (0, h))


def per_head(*dims):
    return pl.BlockSpec((1,) + dims, lambda h: (h,) + (0,) * len(dims))


def per_chunk_head(chunks, *dims):
    return pl.BlockSpec((chunks, 1) + dims, lambda h: (0, h) + (0,) * len(dims))


def positions():
    row = lax.broadcasted_iota(jnp.int32, (C, C), 0)
    column = lax.broadcasted_iota(jnp.int32, (C, C), 1)
    return row, column


CUM, BETA, LEAD, CLOSE, COUNT = 0, 1, 2, 3, 4


def ratios_of(cols, rows, at):
    row, column = positions()
    spread = cols[0, at, CUM : CUM + 1] - rows[0, CUM : CUM + 1, at]
    same = cols[0, at, COUNT : COUNT + 1] == rows[0, COUNT : COUNT + 1, at]
    return jnp.where(same & (row >= column), jnp.exp(jnp.minimum(spread, 0.0)), 0.0)


def mixes_kernel(q, k, cols, rows, lower, within):
    row, column = positions()
    for c in range(q.shape[0] // C):
        at = pl.ds(c * C, C)
        key = k[at, :]
        dots = dot3(jnp.concatenate([key, q[at, :]], 0), key, NT)
        ratios = ratios_of(cols, rows, at)
        lower[c, 0] = jnp.where(row > column, ratios, 0.0) * dots[:C]
        within[c, 0] = ratios * dots[C:]


def inverse_kernel(lower, inverse):
    lanes = lower.shape[2]
    inverse[...] = jnp.zeros(inverse.shape, F32)
    for base in range(0, C, 4):
        width = (base + 4 + 7) // 8 * 8
        place = lax.broadcasted_iota(jnp.int32, (width, lanes), 0)
        found = tuple(jnp.where(place == base + n, 1.0, 0.0).astype(F32) for n in range(4))

        def earlier(j, found):
            known = inverse[j, :width, :]
            return tuple(f - lower[base + n, pl.ds(j, 1), :] * known for n, f in enumerate(found))

        if base:
            found = lax.fori_loop(0, base, earlier, found, unroll=4)
        done = []
        for n in range(4):
            one = found[n]
            for m in range(n):
                one = one - lower[base + n, base + m : base + m + 1, :] * done[m]
            done.append(one)
            inverse[base + n, :width, :] = one


def pieces_kernel(q, k, v, cols, rows, inv, within, u_out, w_out, qm_out, trans_out, a_out, b_out):
    row = lax.broadcasted_iota(jnp.int32, (DK, DK), 0)
    column = lax.broadcasted_iota(jnp.int32, (DK, DK), 1)
    carried = None
    for c in range(q.shape[0] // C):
        at = pl.ds(c * C, C)
        beta, lead = cols[0, at, BETA : BETA + 1], cols[0, at, LEAD : LEAD + 1]
        close = cols[0, at, CLOSE : CLOSE + 1]
        last = cols[0, c * C + C - 1 : c * C + C, LEAD : LEAD + 1]
        key = k[at, :]
        solved = dot3(inv[c, 0], jnp.concatenate([v[at, :], lead * key], 1))
        mix = within[c, 0] * rows[0, BETA : BETA + 1, at]
        w = solved[:, DV:]
        u_out[at, :] = solved[:, :DV]
        w_out[at, :] = w
        qm_out[at, :] = lead * q[at, :] - dot3(mix, w)
        both = dot3(close * beta * key, solved, TN)
        trans = jnp.where(row == column, last, 0.0) - both[:, DV:]
        trans_out[c, 0] = trans
        if carried is None:
            carried = jnp.concatenate([both[:, :DV], trans], 1)
        else:
            carried = dot3(trans, carried)
            carried = jnp.concatenate([carried[:, :DV] + both[:, :DV], carried[:, DV:]], 1)
    b_out[0] = carried[:, :DV]
    a_out[0] = carried[:, DV:]


def outputs_kernel(s_in, q, k, u, w, cols, rows, within, out, residue, states):
    state = s_in[0]
    for c in range(q.shape[0] // C):
        at = pl.ds(c * C, C)
        beta, lead = cols[0, at, BETA : BETA + 1], cols[0, at, LEAD : LEAD + 1]
        close = cols[0, at, CLOSE : CLOSE + 1]
        last = cols[0, c * C + C - 1 : c * C + C, LEAD : LEAD + 1]
        states[c, 0] = state
        read = dot3(jnp.concatenate([w[at, :], lead * q[at, :]], 0), state)
        left = u[at, :] - read[:C]
        residue[at, :] = left
        out[at, :] = read[C:] + dot3(within[c, 0] * rows[0, BETA : BETA + 1, at], left)
        state = last * state + dot3(close * beta * k[at, :], left, TN)


def adjoint_piece_kernel(qm, d_out, trans, direct):
    carried = None
    for c in reversed(range(qm.shape[0] // C)):
        at = pl.ds(c * C, C)
        here = dot3(qm[at, :], d_out[at, :], TN)
        carried = here if carried is None else here + dot3(trans[c, 0], carried, TN)
    direct[0] = carried


def adjoint_kernel(
    z_in, q, k, cols, rows, inv, lower, within, residue, states, d_out,
    dq, dk, dv, dcols, drows,
):
    z = z_in[0]
    row, column = positions()
    for c in reversed(range(q.shape[0] // C)):
        at = pl.ds(c * C, C)
        beta, lead = cols[0, at, BETA : BETA + 1], cols[0, at, LEAD : LEAD + 1]
        close = cols[0, at, CLOSE : CLOSE + 1]
        last = cols[0, c * C + C - 1 : c * C + C, LEAD : LEAD + 1]
        beta_row = rows[0, BETA : BETA + 1, at]
        key, query, left, state = k[at, :], q[at, :], residue[at, :], states[c, 0]
        ratios = ratios_of(cols, rows, at)
        grad = d_out[at, :]
        d_left = dot3(within[c, 0] * beta_row, grad, TN) + dot3(close * beta * key, z)
        e = dot3(inv[c, 0], d_left, TN)
        dv[at, :] = e
        both = jnp.concatenate([grad, e], 0)
        back = dot3(both, state, NT)
        d_mix = dot3(both, left, NT)
        d_within = jnp.where(row >= column, d_mix[:C], 0.0)
        d_lower = jnp.where(row > column, -d_mix[C:], 0.0)
        d_close = dot3(left, z, NT)
        d_last = jnp.sum(z * state)
        z = last * z + dot3(jnp.concatenate([lead * query, -lead * key], 0), both, TN)
        of_query = d_within * ratios * beta_row
        of_key = d_lower * ratios * beta_row
        pair = jnp.concatenate([of_query, of_key], 0)
        forth = dot3(pair, key)
        dq[at, :] = lead * back[:C] + forth[:C]
        dk[at, :] = (
            close * beta * d_close
            - lead * back[C:]
            + forth[C:]
            + dot3(pair, jnp.concatenate([query, key], 0), TN)
        )
        share = d_within * within[c, 0] + d_lower * lower[c, 0]
        drows[0, 0:1, at] = jnp.sum(share, 0, keepdims=True)
        dcols[0, at, 0:1] = jnp.sum(share * beta_row, 1, keepdims=True)
        dcols[0, at, 1:2] = jnp.sum(key * d_close, 1, keepdims=True)
        dcols[0, at, 2:3] = jnp.sum(back[:C] * query - back[C:] * key, 1, keepdims=True)
        dcols[0, at, 3:4] = jnp.full((C, 1), d_last, F32)


def states_kernel(me, maps, out):
    count = maps.shape[0]
    state = jnp.zeros((DK, DV), F32)
    for piece in range(count):
        slot = piece ^ me[0]
        out[slot] = state
        if piece < count - 1:
            held = maps[slot]
            state = dot3(held[:, DV:], state) + held[:, :DV]


def adjoints_kernel(me, maps, direct, out):
    count = maps.shape[0]
    z = jnp.zeros((DK, DV), F32)
    for piece in reversed(range(count)):
        slot = piece ^ me[0]
        out[slot] = z
        if piece:
            z = dot3(maps[slot][:, DV:], z, TN) + direct[slot]


def whole_call(kernel, me, args, out_shape, name):
    return pl.pallas_call(
        kernel,
        grid_spec=pltpu.PrefetchScalarGridSpec(
            num_scalar_prefetch=1,
            grid=(1,),
            in_specs=[pl.BlockSpec(a.shape, lambda i, me: (0, 0, 0)) for a in args],
            out_specs=pl.BlockSpec(out_shape.shape, lambda i, me: (0, 0, 0)),
        ),
        out_shape=out_shape,
        name=name,
        compiler_params=pltpu.CompilerParams(vmem_limit_bytes=VMEM_BYTES),
    )(me.reshape(1), *args)


def heads_apart(whole, me):
    parts = [lax.dynamic_index_in_dim(whole, me, 0, False)]
    for r in range(1, whole.shape[0]):
        parts.append(swapped(lax.dynamic_index_in_dim(whole, me ^ r, 0, False), "seq", r))
    return jnp.stack(parts)


def heads_together(parts, me):
    count = parts.shape[0]
    held = jnp.stack([parts[0]] + [swapped(parts[r], "seq", r) for r in range(1, count)])
    return held[jnp.arange(count) ^ me]


def compose(earlier, later):
    first = jnp.einsum("hij,hjk->hik", later[0], earlier[0], precision=lax.Precision.HIGHEST)
    second = jnp.einsum("hij,hjk->hik", later[0], earlier[1], precision=lax.Precision.HIGHEST)
    return (first, second + later[1])


def entering(part, reverse):
    count, place = lax.axis_size("seq"), lax.axis_index("seq")
    ahead = count - 1 - place if reverse else place
    gathered = jax.tree.map(lambda a: lax.all_gather(a, "seq"), part)
    state = (jnp.broadcast_to(jnp.eye(DK, dtype=F32), part[0].shape), jnp.zeros_like(part[1]))

    def one(step, state):
        source = count - 1 - step if reverse else step
        here = jax.tree.map(lambda a: lax.dynamic_index_in_dim(a, source, 0, False), gathered)
        return compose(state, here)

    return lax.fori_loop(0, ahead, one, state)[1]


def on_device(
    residual_in, doc_starts, out_grad, norm_gain, qkv_weight, gate_weight, decay_beta_weight,
    conv_weight, decay_log, decay_bias, beta_bias, head_gain, out_weight, mlp_gain, up_weight,
    down_weight,
):
    place, piece = lax.axis_index("fsdp"), lax.axis_index("seq")
    pieces = lax.axis_size("seq")
    bits = [(piece >> s) & 1 for s in range(pieces.bit_length() - 1)]
    bit = bits[0]
    rows, starts, cotangent = residual_in[0], doc_starts[0], out_grad[0]
    tokens = rows.shape[0]
    chunks = tokens // C

    small = [norm_gain, decay_beta_weight, conv_weight, decay_log, decay_bias, beta_bias, head_gain, mlp_gain]
    sizes = [a.size for a in small]
    packed = jnp.concatenate([a.reshape(-1) for a in small])
    held = jnp.stack([packed] + [swapped(packed, "fsdp", r) for r in range(1, 4)])
    held = held[jnp.arange(4) ^ place]
    parts, offset = [], 0
    for a, size in zip(small, sizes):
        parts.append(held[:, offset : offset + size].reshape((4,) + a.shape))
        offset += size
    full_norm, full_decay_beta = parts[0].reshape(-1), parts[1].reshape(D, 2 * H)
    full_conv = jnp.transpose(parts[2], (1, 0, 2)).reshape(CONV, -1)
    full_decay_log, full_decay_bias, full_beta_bias = (parts[i].reshape(-1) for i in (3, 4, 5))
    full_head_gain, full_mlp_gain = parts[6].reshape(-1), parts[7].reshape(-1)

    qkv = gathered_weight(qkv_weight, bit)
    gate = gathered_weight(gate_weight, bit)
    out_w = gathered_weight(out_weight, bit)
    up = gathered_weight(up_weight, bit)
    down = gathered_weight(down_weight, bit)

    def forward(x, weight):
        starts_ = block_starts(weight[0].shape[0], place, bit)
        x = jnp.concatenate([columns_of(x, at, size) for at, size in starts_], 1)
        return dot(x, jnp.concatenate(weight, 0))

    def backward_rows(dy, weight):
        shard = weight[0].shape[0]
        starts_ = block_starts(shard, place, bit)
        blocks = dot(dy, jnp.concatenate(weight, 0), NT)
        whole, offset = jnp.zeros((tokens, 4 * shard), F32), 0
        for at, size in starts_:
            whole = lax.dynamic_update_slice_in_dim(
                whole, blocks[:, offset : offset + size], at, 1
            )
            offset += size
        return whole

    def weight_grad(x, dy, shard):
        return [dot(columns_of(x, (place ^ r) * shard, shard), dy, TN) for r in range(4)]

    counts = jnp.cumsum(starts)
    after = jnp.flip(jnp.cumsum(jnp.flip(starts))) - starts
    tail_mask = (after[tokens - CONV + 1 :] == 0).astype(F32)[:, None]
    by_chunk = counts.reshape(chunks, C)
    before = (counts - starts).reshape(chunks, C)[:, :1]
    of_lead = (by_chunk == before).astype(F32)
    of_close = (by_chunk == by_chunk[:, -1:]).astype(F32)

    normed, norm_pull = jax.vjp(rms_norm, rows, full_norm)
    mixed_in = forward(normed, qkv)
    rim_rows = passed_along(mixed_in[tokens - CONV + 1 :] * tail_mask, "seq", 1)
    decay_beta = dot(normed, full_decay_beta)
    gate_rows = forward(normed, gate)
    front_parts, front_pull = jax.vjp(
        partial(front, counts=counts),
        mixed_in, rim_rows, decay_beta, full_conv, full_decay_log, full_decay_bias, full_beta_bias,
    )
    queries, key_rows, values, log_decay, beta = front_parts

    cum = jnp.cumsum(log_decay.reshape(chunks, C, H), 1)
    lead = jnp.exp(cum) * of_lead[:, :, None]
    close = jnp.exp(cum[:, -1:] - cum) * of_close[:, :, None]
    count_cols = jnp.broadcast_to(counts.astype(F32)[:, None], (tokens, H))
    flat = [a.reshape(tokens, H) for a in (cum, beta, lead, close)] + [count_cols]
    rows_in = jnp.stack([a.T for a in flat], 1)
    rows_in = jnp.concatenate([rows_in, jnp.zeros((H, 3, tokens), F32)], 1)
    cols_in = jnp.transpose(rows_in, (0, 2, 1))

    key_spec, value_spec = head_block(tokens, DK), head_block(tokens, DV)
    cols_spec, rows_spec = per_head(tokens, 8), per_head(8, tokens)
    square_spec = per_chunk_head(chunks, C, C)
    state_spec = per_chunk_head(chunks, DK, DV)
    square = shape(chunks, H, C, C)
    lower, within = call(
        mixes_kernel, (H,),
        [key_spec, key_spec, cols_spec, rows_spec],
        [square_spec, square_spec], [square, square], name="mixes",
    )(queries, key_rows, cols_in, rows_in)
    lower_mix = lower * rows_in[:, BETA, :].reshape(H, chunks, C).transpose(1, 0, 2)[:, :, None, :]
    lanes = jnp.transpose(lower_mix.reshape(chunks * H, C, C), (1, 2, 0))
    inverse = pl.pallas_call(
        inverse_kernel,
        out_shape=shape(C, C, chunks * H),
        name="inverse",
        compiler_params=pltpu.CompilerParams(vmem_limit_bytes=VMEM_BYTES),
    )(lanes)
    inverse = jnp.transpose(inverse, (2, 0, 1)).reshape(chunks, H, C, C)
    solved_values, solved_keys, query_map, trans, map_a, map_b = call(
        pieces_kernel, (H,),
        [key_spec, key_spec, value_spec, cols_spec, rows_spec, square_spec, square_spec],
        [value_spec, key_spec, key_spec, per_chunk_head(chunks, DK, DK), per_head(DK, DK), per_head(DK, DV)],
        [shape(tokens, H * DV), shape(tokens, H * DK), shape(tokens, H * DK),
         shape(chunks, H, DK, DK), shape(H, DK, DK), shape(H, DK, DV)],
        name="pieces",
    )(queries, key_rows, values, cols_in, rows_in, inverse, within)

    spread = pieces == H
    if spread:
        maps = heads_apart(jnp.concatenate([map_b, map_a], 2), piece)
        incoming = whole_call(states_kernel, piece, [maps], shape(H, DK, DV), "states")
        state_in = heads_together(incoming, piece)
    else:
        state_in = entering((map_a, map_b), False)
    head_outputs, residues, states = call(
        outputs_kernel, (H,),
        [per_head(DK, DV), key_spec, key_spec, value_spec, key_spec, cols_spec, rows_spec, square_spec],
        [value_spec, value_spec, state_spec],
        [shape(tokens, H * DV), shape(tokens, H * DV), shape(chunks, H, DK, DV)],
        name="outputs",
    )(state_in, queries, key_rows, solved_values, solved_keys, cols_in, rows_in, within)

    gated, gated_pull = jax.vjp(gate_heads, head_outputs, gate_rows, full_head_gain)
    mixer = forward(gated, out_w)
    middle = rows + mixer
    lifted_in, lifted_pull = jax.vjp(rms_norm, middle, full_mlp_gain)
    lifted = forward(lifted_in, up)
    hidden, hidden_pull = jax.vjp(swiglu, lifted)
    branch = forward(hidden, down)
    result = middle + branch
    squares = jnp.stack([jnp.sum(a * a) for a in (rows, mixer, branch, result)])

    grad_down = reduced_shard(weight_grad(hidden, cotangent, FF // 4), bits)
    (d_lifted,) = hidden_pull(backward_rows(cotangent, down))
    grad_up = reduced_shard(weight_grad(lifted_in, d_lifted, D // 4), bits)
    d_middle, grad_mlp_gain = lifted_pull(backward_rows(d_lifted, up))
    d_middle = d_middle + cotangent
    grad_out = reduced_shard(weight_grad(gated, d_middle, H * DV // 4), bits)
    d_heads, d_gate, grad_head_gain = gated_pull(backward_rows(d_middle, out_w))
    grad_gate = reduced_shard(weight_grad(normed, d_gate, D // 4), bits)

    direct = call(
        adjoint_piece_kernel, (H,),
        [key_spec, value_spec, per_chunk_head(chunks, DK, DK)],
        per_head(DK, DV), shape(H, DK, DV), name="adjoint_piece",
    )(query_map, d_heads, trans)
    if spread:
        outgoing = whole_call(
            adjoints_kernel, piece, [maps, heads_apart(direct, piece)], shape(H, DK, DV), "adjoints"
        )
        adjoint_in = heads_together(outgoing, piece)
    else:
        adjoint_in = entering((jnp.swapaxes(map_a, 1, 2), direct), True)
    d_queries, d_keys, d_values, dcols, drows = call(
        adjoint_kernel, (H,),
        [per_head(DK, DV), key_spec, key_spec, cols_spec, rows_spec, square_spec, square_spec,
         square_spec, value_spec, state_spec, value_spec],
        [key_spec, key_spec, value_spec, cols_spec, rows_spec],
        [shape(tokens, H * DK), shape(tokens, H * DK), shape(tokens, H * DV),
         shape(H, tokens, 8), shape(H, 8, tokens)],
        name="adjoint",
    )(adjoint_in, queries, key_rows, cols_in, rows_in, inverse, lower, within, residues, states, d_heads)

    def by_token(a):
        return a.T.reshape(chunks, C, H)

    of_share, of_row = by_token(drows[:, 0, :]), by_token(dcols[:, :, 0])
    of_closing, of_leading = by_token(dcols[:, :, 1]), by_token(dcols[:, :, 2])
    of_last = by_token(dcols[:, :, 3])[:, -1:]
    beta_ = beta.reshape(chunks, C, H)
    d_beta = of_share + close * of_closing
    closing = close * beta_ * of_closing
    d_cum = of_row - beta_ * of_share + lead * of_leading - closing
    ending = jnp.sum(closing, 1, keepdims=True) + lead[:, -1:] * of_last
    d_cum = d_cum + jnp.pad(ending, ((0, 0), (C - 1, 0), (0, 0)))
    d_log = jnp.flip(jnp.cumsum(jnp.flip(d_cum, 1), 1), 1)

    (d_mixed, d_rim, d_decay_beta, grad_conv, grad_decay_log, grad_decay_bias, grad_beta_bias) = (
        front_pull(
            (d_queries, d_keys, d_values, d_log.reshape(tokens, H), d_beta.reshape(tokens, H))
        )
    )
    returned = passed_along(d_rim, "seq", -1)
    d_mixed = d_mixed.at[tokens - CONV + 1 :].add(returned * tail_mask)
    grad_qkv = reduced_shard(weight_grad(normed, d_mixed, D // 4), bits)
    grad_decay_beta = dot(normed, d_decay_beta, TN)
    d_normed = (
        backward_rows(d_mixed, qkv)
        + backward_rows(d_gate, gate)
        + dot(d_decay_beta, full_decay_beta, NT)
    )
    d_rows, grad_norm = norm_pull(d_normed)
    row_grad = d_rows + d_middle

    small_grads = [
        grad_norm.reshape(4, -1),
        grad_decay_beta.reshape(4, -1),
        jnp.transpose(grad_conv.reshape(CONV, 4, -1), (1, 0, 2)).reshape(4, -1),
        grad_decay_log.reshape(4, -1),
        grad_decay_bias.reshape(4, -1),
        grad_beta_bias.reshape(4, -1),
        grad_head_gain.reshape(4, -1),
        grad_mlp_gain.reshape(4, -1),
        jnp.broadcast_to(squares, (4, 4)),
    ]
    rows4 = jnp.concatenate(small_grads, 1)[jnp.arange(4) ^ place]
    summed = summed_small(rows4, bits)
    out_small, offset = [], 0
    for a, size in zip(small, sizes):
        out_small.append(summed[offset : offset + size].reshape(a.shape))
        offset += size
    rms_values = jnp.sqrt(summed[offset:] / (pieces * lax.axis_size("fsdp") * tokens * D))

    return (
        result[None],
        row_grad[None],
        out_small[0],
        grad_qkv,
        grad_gate,
        out_small[1],
        out_small[2],
        out_small[3],
        out_small[4],
        out_small[5],
        out_small[6],
        grad_out,
        out_small[7],
        grad_up,
        grad_down,
        rms_values,
    )


def solution(mesh):
    split_tokens = P("fsdp", "seq", None)
    lines = P("fsdp", None)
    return jax.shard_map(
        on_device,
        mesh=mesh,
        in_specs=(
            split_tokens, P("fsdp", "seq"), split_tokens, P("fsdp"), lines, lines, lines,
            P(None, "fsdp"), P("fsdp"), P("fsdp"), P("fsdp"), P("fsdp"), lines, P("fsdp"), lines, lines,
        ),
        out_specs=(
            split_tokens, split_tokens, P("fsdp"), lines, lines, lines, P(None, "fsdp"),
            P("fsdp"), P("fsdp"), P("fsdp"), P("fsdp"), lines, P("fsdp"), lines, lines, P(),
        ),
        check_vma=False,
    )
```

```python
from functools import partial

import jax
import jax.numpy as jnp
from jax import lax
from jax.experimental import pallas as pl
from jax.experimental.pallas import tpu as pltpu
from jax.sharding import PartitionSpec as P

D = 1024
H = 8
DK = 128
DV = 256
FF = 2816
CONV = 4
C = 64
FSDP, SEQ = "fsdp", "seq"
RIM = 16
PAIR = 2

NORM_EPS = 1e-05
UNIT_EPS = 1e-06
F32 = jnp.float32
BF16 = jnp.bfloat16
VMEM_BYTES = 56 * 1024 * 1024

NN = (((1,), (0,)), ((), ()))
NT = (((1,), (1,)), ((), ()))
TN = (((0,), (0,)), ((), ()))


def swapped(block, axis, distance):
    return lax.ppermute(block, axis, [(i, i ^ distance) for i in range(lax.axis_size(axis))])


def passed_along(block, axis, distance):
    devices = range(lax.axis_size(axis))
    route = [(i - distance, i) for i in devices if i - distance in devices]
    return lax.ppermute(block, axis, route)


def rows_of(block, start, size):
    return lax.dynamic_slice_in_dim(block, start, size, 0)


class Free:
    def gate(self, value):
        return value

    def wait(self, *done):
        pass

    def send(self, block, axis, distance):
        return swapped(block, axis, distance)


class Clock:
    def __init__(self):
        self.token = jnp.zeros((8, 128), F32)

    def wait(self, *done):
        self.token = lax.optimization_barrier((self.token,) + done)[0]

    def gate(self, value):
        return lax.optimization_barrier((value, self.token))[0]

    def send(self, block, axis, distance):
        return swapped(self.gate(block), axis, distance)

    def run(self, kernel, first, *rest):
        found = kernel(self.gate(first), *rest)
        self.wait(found[0] if isinstance(found, (list, tuple)) else found)
        return found


class Transfer:
    def __init__(self, clock, source, move):
        self.clock, self.source, self.move = clock, source, move

    def start(self):
        self.come = self.move(self.clock.gate(self.source()))

    def wait(self):
        self.clock.wait(self.come)


def swap(axis, distance):
    return lambda block: swapped(block, axis, distance)


def couples():
    return [[i, i + 1] for i in range(0, lax.axis_size(FSDP), 2)]


class Whole:
    def __init__(self, clock, shard):
        self.shard = shard
        self.near = Transfer(
            clock,
            lambda: shard,
            lambda a: lax.all_gather(a, FSDP, axis=0, tiled=True, axis_index_groups=couples()),
        )


class Piece:
    def __init__(self, clock, whole, column, width, step, bits, place):
        self.clock, self.whole, self.column, self.width = clock, whole, column, width
        self.bit, self.place = bits[min(step, len(bits) - 1)], place
        half = whole.shard.shape[0] // 2
        self.own = lax.dynamic_slice(whole.shard, (self.bit * half, column), (half, width))
        step = min(step, len(bits) - 1)
        self.far = Transfer(clock, lambda: self.own, swap(FSDP, 2))
        self.side = Transfer(clock, lambda: self.far.come, swap(SEQ, 1 << step))
        self.last_a = Transfer(clock, lambda: self.far.come, swap(FSDP, 1))
        self.last_b = Transfer(clock, lambda: self.side.come, swap(FSDP, 1))

    def weight(self):
        shard, place = self.whole.shard.shape[0], self.place
        half = shard // 2
        blocks = [self.whole.near.come] + [
            t.come for t in (self.far, self.side, self.last_a, self.last_b)
        ]
        starts = [(place & 2) * shard] + [
            (place ^ r) * shard + (self.bit ^ part) * half for r in (2, 3) for part in range(2)
        ]
        return Weight(blocks, [self.column] + [0] * 4, self.width, [1] * 5, jnp.stack(starts))

    def pack(self, tile, us):
        weight = self.weight()
        weight.blocks[0] = self.clock.gate(weight.blocks[0])
        self.packed = packed_weight(weight, tile, us)
        self.clock.wait(*self.packed)


class SmallSum:
    def __init__(self, clock, rows4, bits):
        self.clock, self.rows, self.at, self.count = clock, rows4, 0, len(bits)

    def start(self):
        block = (self.rows[1::2], self.rows[1:])[self.at] if self.at < 2 else self.rows
        axis, distance = (FSDP, 1 << self.at) if self.at < 2 else (SEQ, 1 << (self.at - 2))
        self.come = self.clock.send(block, axis, distance)

    def wait(self):
        self.clock.wait(self.come)
        kept = (self.rows[0::2], self.rows[:1])[self.at] if self.at < 2 else self.rows
        self.rows, self.at = kept + self.come, self.at + 1

    def finish(self):
        self.clock = Free()
        while self.at < 2 + self.count:
            self.start()
            self.wait()
        return self.rows[0]


def split(x):
    high = x.astype(BF16)
    return high, (x - high.astype(F32)).astype(BF16)


def one_pass(left, right, dims=NN):
    return lax.dot_general(left, right, dims, preferred_element_type=F32)


def dot_halves(lh, ll, rh, rl, dims=NN):
    return one_pass(lh, rh, dims) + (one_pass(lh, rl, dims) + one_pass(ll, rh, dims))


def stacked(ref, x):
    rows = x.shape[0]
    ref[:rows], ref[rows:] = split(x)


def dot_stacked(left, high, low, dims=NN):
    rows = left.shape[0] // 2
    top = one_pass(left[...], high, dims)
    return top[:rows] + (top[rows:] + one_pass(left[:rows], low, dims))


def dot3(left, right, dims=NN):
    return dot_halves(*split(left), *split(right), dims)


def dot3c(left, right, dims=NN):
    (one,), (two,) = dims[0]
    lh, ll = split(left)
    rh, rl = split(right)
    left = jnp.concatenate([lh, lh, ll], one)
    right = jnp.concatenate([rh, rl, rh], two)
    return lax.dot_general(left, right, dims, preferred_element_type=F32)


def dot(left, right, dims=NN):
    return lax.dot_general(
        left, right, dims, precision=lax.Precision.HIGH, preferred_element_type=F32
    )


def shape(*dims):
    return jax.ShapeDtypeStruct(dims, F32)


def cost(us):
    return pl.CostEstimate(flops=int(us), bytes_accessed=1024, transcendentals=0)


def call(kernel, grid, in_specs, out_specs, out_shape, name, us, scratch=(), prefetch=0):
    return pl.pallas_call(
        kernel,
        grid_spec=pltpu.PrefetchScalarGridSpec(
            num_scalar_prefetch=prefetch,
            grid=grid,
            in_specs=in_specs,
            out_specs=out_specs,
            scratch_shapes=scratch,
        ),
        out_shape=out_shape,
        name=name,
        compiler_params=pltpu.CompilerParams(
            vmem_limit_bytes=VMEM_BYTES, dimension_semantics=("arbitrary",) * len(grid)
        ),
        cost_estimate=cost(us),
    )


def fixed(array):
    return pl.BlockSpec(array.shape, lambda j, *_: (0,) * len(array.shape))


class Weight:
    def __init__(self, blocks, columns, width, parts, starts):
        self.blocks, self.columns, self.width = blocks, columns, width
        self.parts, self.starts = parts, starts

    def specs(self, tile):
        return [
            pl.BlockSpec((block.shape[0], tile), lambda j, *_, shift=column // tile: (0, j + shift))
            for block, column in zip(self.blocks, self.columns)
        ]


def place_weight(starts, refs, parts, high, low, columns):
    n = 0
    for ref, count in zip(refs, parts):
        size = ref.shape[0] // count
        for part in range(count):
            at = pl.ds(pl.multiple_of(starts[n], 16), size)
            high[at, columns], low[at, columns] = split(ref[part * size : (part + 1) * size])
            n += 1


def block_product(x, weight, tile, name, us):
    tokens, depth = x.shape
    width = weight.width
    count = len(weight.blocks)

    def kernel(starts, x_ref, *refs):
        blocks, refs = refs[:count], refs[count:]
        out, xs, wh, wl = refs

        @pl.when(pl.program_id(0) == 0)
        def _():
            stacked(xs, x_ref[...])

        place_weight(starts, blocks, weight.parts, wh, wl, slice(None))
        out[...] = dot_stacked(xs, wh[...], wl[...])

    tiled = pl.BlockSpec((tokens, tile), lambda j, *_: (0, j))
    return call(
        kernel,
        (width // tile,),
        [fixed(x)] + weight.specs(tile),
        tiled,
        shape(tokens, width),
        name,
        us,
        [pltpu.VMEM((2 * tokens, depth), BF16)] + [pltpu.VMEM((depth, tile), BF16)] * 2,
        prefetch=1,
    )(weight.starts, x, *weight.blocks)


def block_product_back(parts, tile, name, us, add=None):
    tokens, width = parts[0][0].shape[-2:]
    depth = 2 * parts[0][1].blocks[0].shape[0]
    count = len(parts[0][1].blocks)
    planes = parts[0][0].ndim == 3
    steps = width // tile
    n = len(parts)

    def kernel(starts, *refs):
        dys, refs = refs[: 1 if planes else n], refs[1 if planes else n :]
        blocks, refs = refs[: n * count], refs[n * count :]
        if add is not None:
            add_ref, refs = refs[0], refs[1:]
        out, wh, wl = refs
        for p in range(n):
            columns = slice(p * tile, (p + 1) * tile)
            refs_ = blocks[p * count : (p + 1) * count]
            place_weight(starts, refs_, parts[p][1].parts, wh, wl, columns)
        dy = jnp.concatenate([dys[0][p] for p in range(n)], 1) if planes else dys[0][...]
        found = dot_halves(*split(dy), wh[...], wl[...], NT)

        @pl.when(pl.program_id(0) == 0)
        def _():
            out[...] = found if add is None else found + add_ref[...]

        @pl.when(pl.program_id(0) > 0)
        def _():
            out[...] += found

    tiled = pl.BlockSpec((tokens, tile), lambda j, *_: (0, j))
    whole = pl.BlockSpec((tokens, depth), lambda j, *_: (0, 0))
    specs, arrays = [tiled], [parts[0][0]]
    if planes:
        specs = [pl.BlockSpec((n, tokens, tile), lambda j, *_: (0, 0, j))]
    for _, weight in parts:
        specs += weight.specs(tile)
        arrays += weight.blocks
    if add is not None:
        specs, arrays = specs + [whole], arrays + [add]
    return call(
        kernel, (steps,), specs, whole, shape(tokens, depth), name, us,
        [pltpu.VMEM((depth, n * tile), BF16)] * 2, prefetch=1,
    )(parts[0][1].starts, *arrays)


def packed_weight(weight, tile, us):
    depth, width = 2 * weight.blocks[0].shape[0], weight.width

    def kernel(starts, *refs):
        place_weight(starts, refs[:-2], weight.parts, *refs[-2:], slice(None))

    return call(
        kernel,
        (width // tile,),
        weight.specs(tile),
        [pl.BlockSpec((depth, tile), lambda j, *_: (0, j))] * 2,
        [jax.ShapeDtypeStruct((depth, width), BF16)] * 2,
        "packed",
        us,
        prefetch=1,
    )(weight.starts, *weight.blocks)


def product(x, weight, tile, name, us):
    tokens, depth = x.shape
    width = weight[0].shape[1]

    def kernel(x_ref, high, low, out, xs):
        @pl.when(pl.program_id(0) == 0)
        def _():
            stacked(xs, x_ref[...])

        out[...] = dot_stacked(xs, high[...], low[...])

    tiled = pl.BlockSpec((tokens, tile), lambda j: (0, j))
    weights = pl.BlockSpec((depth, tile), lambda j: (0, j))
    return call(
        kernel, (width // tile,), [fixed(x), weights, weights], tiled, shape(tokens, width),
        name, us, [pltpu.VMEM((2 * tokens, depth), BF16)],
    )(x, *weight)


def lifted_product(x, weight_a, weight_b, tile, us):
    tokens, depth = x.shape

    def kernel(x_ref, ah, al, bh, bl, a_out, b_out, hidden, xs):
        @pl.when(pl.program_id(0) == 0)
        def _():
            stacked(xs, x_ref[...])

        a = dot_stacked(xs, ah[...], al[...])
        b = dot_stacked(xs, bh[...], bl[...])
        a_out[...] = a
        b_out[...] = b
        hidden[...] = a * jax.nn.sigmoid(a) * b

    tiled = pl.BlockSpec((tokens, tile), lambda j: (0, j))
    weights = pl.BlockSpec((depth, tile), lambda j: (0, j))
    return call(
        kernel, (FF // tile,), [fixed(x)] + [weights] * 4, [tiled] * 3, [shape(tokens, FF)] * 3,
        "lifted", us, [pltpu.VMEM((2 * tokens, depth), BF16)],
    )(x, *weight_a, *weight_b)


def product_back(dy, weight, tile, name, us, add=None):
    tokens, width = dy.shape
    depth = weight[0].shape[0]

    def kernel(dy_ref, high, low, *refs):
        out, ds = refs[-2:]

        @pl.when(pl.program_id(0) == 0)
        def _():
            stacked(ds, dy_ref[...])

        found = dot_stacked(ds, high[...], low[...], NT)
        out[...] = found if add is None else found + refs[0][...]

    tiled = pl.BlockSpec((tokens, tile), lambda j: (0, j))
    weights = pl.BlockSpec((tile, width), lambda j: (j, 0))
    more = [] if add is None else [add]
    return call(
        kernel, (depth // tile,), [fixed(dy), weights, weights] + [tiled] * len(more), tiled,
        shape(tokens, depth), name, us, [pltpu.VMEM((2 * tokens, width), BF16)],
    )(dy, *weight, *more)


def hidden_back(dy, weight, a, b, tile, us):
    tokens, width = dy.shape

    def kernel(dy_ref, high, low, a_ref, b_ref, d_a, d_b, ds):
        @pl.when(pl.program_id(0) == 0)
        def _():
            stacked(ds, dy_ref[...])

        found = dot_stacked(ds, high[...], low[...], NT)
        opened = jax.nn.sigmoid(a_ref[...])
        d_a[...] = found * b_ref[...] * opened * (1.0 + a_ref[...] * (1.0 - opened))
        d_b[...] = found * a_ref[...] * opened

    tiled = pl.BlockSpec((tokens, tile), lambda j: (0, j))
    weights = pl.BlockSpec((tile, width), lambda j: (j, 0))
    return call(
        kernel, (FF // tile,), [fixed(dy), weights, weights, tiled, tiled], [tiled] * 2,
        [shape(tokens, FF)] * 2, "hidden_back", us, [pltpu.VMEM((2 * tokens, width), BF16)],
    )(dy, *weight, a, b)


def weight_grad(x, dy, halves, groups, tile, name, us, add=None):
    tokens, depth = x.shape
    half, count = depth // 8, halves.shape[0]
    planes = dy.ndim == 3
    width = dy.shape[0] * dy.shape[2] if planes else dy.shape[1]
    size = count * half // groups

    def kernel(halves, x_ref, dy_ref, *refs):
        adds, refs = (refs[:groups], refs[groups:]) if add is not None else ((), refs)
        outs, (xt, xs) = refs[:groups], refs[groups:]

        @pl.when(pl.program_id(0) == 0)
        def _():
            xt[...] = x_ref[...].T
            for n in range(count):
                high, low = split(xt[pl.ds(pl.multiple_of(halves[n], 16), half), :])
                xs[n * half : (n + 1) * half] = high
                xs[(count + n) * half : (count + n + 1) * half] = low

        found = dot_stacked(xs, *split(dy_ref[0] if planes else dy_ref[...]))
        for n in range(groups):
            block = found[n * size : (n + 1) * size]
            outs[n][...] = block + adds[n][...] if adds else block

    tiled = pl.BlockSpec((size, tile), lambda j, *_: (0, j))
    added = [pl.BlockSpec((size, tile), lambda j, *_, n=n: (n, j)) for n in range(groups)]
    of_dy = pl.BlockSpec((tokens, tile), lambda j, *_: (0, j))
    if planes:
        each = dy.shape[2] // tile
        of_dy = pl.BlockSpec((1, tokens, tile), lambda j, *_: (j // each, 0, j % each))
    more = [add] * groups if add is not None else []
    return call(
        kernel,
        (width // tile,),
        [fixed(x), of_dy] + added[: len(more)],
        [tiled] * groups,
        [shape(size, width)] * groups,
        name,
        us,
        [pltpu.VMEM((depth, tokens), F32), pltpu.VMEM((2 * count * half, tokens), BF16)],
        prefetch=1,
    )(halves, x, dy, *more)


def rms_norm(rows, gain):
    return rows * lax.rsqrt(jnp.mean(rows * rows, axis=-1, keepdims=True) + NORM_EPS) * gain


def scalars_of(decay_beta, decay_log, decay_bias, beta_bias):
    log_decay = -jnp.exp(decay_log) * jax.nn.softplus(decay_beta[:, :H] + decay_bias)
    return log_decay, jax.nn.sigmoid(decay_beta[:, H:] + beta_bias)


def total(x, axis):
    return jnp.sum(x, axis, keepdims=True)


def unit(x):
    return lax.rsqrt(total(x * x, 1) + UNIT_EPS)


def convolved(mixed, taps, same):
    tokens = mixed.shape[0] - RIM
    found = taps[0:1] * mixed[RIM:]
    for s in range(1, CONV):
        found = found + taps[s : s + 1] * (mixed[RIM - s : RIM - s + tokens] * same[:, s : s + 1])
    return found


def convolved_back(d_act, mixed, taps, same, d_mixed, d_rim, d_taps):
    tokens, width = d_act.shape
    before = convolved(mixed, taps, same)
    gate = jax.nn.sigmoid(before)
    d_before = d_act * gate * (1.0 + before * (1.0 - gate))
    empty = jnp.zeros((RIM, width), F32)
    found = jnp.concatenate([empty, taps[0:1] * d_before], 0)
    d_taps[0:1] = total(d_before * mixed[RIM:], 0)
    for s in range(1, CONV):
        reached = d_before * same[:, s : s + 1]
        padded = jnp.concatenate([empty, reached, empty], 0)
        found = found + taps[s : s + 1] * padded[s : s + RIM + tokens]
        d_taps[s : s + 1] = total(reached * mixed[RIM - s : RIM - s + tokens], 0)
    d_mixed[...] = found[RIM:]
    d_rim[...] = found[:RIM]


def silu(x):
    return x * jax.nn.sigmoid(x)


def heads_block(rows, width, shift=0):
    return pl.BlockSpec((rows, PAIR * width), lambda h, *_: (0, h + shift))


def per_heads(*dims):
    return pl.BlockSpec((PAIR,) + dims, lambda h, *_: (h,) + (0,) * len(dims))


def per_chunk_heads(chunks, *dims):
    return pl.BlockSpec((chunks, PAIR) + dims, lambda h, *_: (0, h) + (0,) * len(dims))


def positions(size=C):
    row = lax.broadcasted_iota(jnp.int32, (size, size), 0)
    column = lax.broadcasted_iota(jnp.int32, (size, size), 1)
    return row, column


CUM, BETA, LEAD, CLOSE, COUNT = 0, 1, 2, 3, 4


class Scalars:
    def __init__(self, cols, rows, p, c):
        at = pl.ds(c * C, C)
        self.at = at
        block, lines = cols[p, at, :], rows[p, :, at]
        self.cum, self.beta = block[:, CUM : CUM + 1], block[:, BETA : BETA + 1]
        self.lead, self.close = block[:, LEAD : LEAD + 1], block[:, CLOSE : CLOSE + 1]
        self.count = block[:, COUNT : COUNT + 1]
        self.last = block[C - 1 : C, LEAD : LEAD + 1]
        self.cum_row, self.beta_row = lines[CUM : CUM + 1], lines[BETA : BETA + 1]
        self.count_row = lines[COUNT : COUNT + 1]

    def ratios(self):
        row, column = positions()
        near = (self.count == self.count_row) & (row >= column)
        return jnp.where(near, jnp.exp(jnp.minimum(self.cum - self.cum_row, 0.0)), 0.0)


def of_head(p, width):
    return slice(p * width, (p + 1) * width)


def keys_kernel(mixed_q, mixed_k, taps_q, taps_k, same, cols, rows, q, k, lower, within, lower_mix):
    row, column = positions()
    for p in range(PAIR):
        of = of_head(p, DK)
        act = silu(convolved(mixed_q[:, of], taps_q[:, of], same))
        q[:, of] = act * unit(act) * DK ** (-0.5)
        act = silu(convolved(mixed_k[:, of], taps_k[:, of], same))
        k[:, of] = act * unit(act)
    for c in range(q.shape[0] // C):
        for p in range(PAIR):
            s, of = Scalars(cols, rows, p, c), of_head(p, DK)
            key = k[s.at, of]
            dots = dot3c(jnp.concatenate([key, q[s.at, of]], 0), key, NT)
            ratios = s.ratios()
            below = jnp.where(row > column, ratios, 0.0) * dots[:C]
            lower[c, p] = below
            lower_mix[c, p] = below * s.beta_row
            within[c, p] = ratios * dots[C:]


def inverse_kernel(lower, inverse):
    lanes = lower.shape[2]
    inverse[...] = jnp.zeros(inverse.shape, F32)
    for base in range(0, C, 4):
        width = (base + 4 + 7) // 8 * 8
        place = lax.broadcasted_iota(jnp.int32, (width, lanes), 0)
        found = tuple(jnp.where(place == base + n, 1.0, 0.0).astype(F32) for n in range(4))

        def earlier(j, found):
            known = inverse[j, :width, :]
            return tuple(f - lower[base + n, pl.ds(j, 1), :] * known for n, f in enumerate(found))

        if base:
            found = lax.fori_loop(0, base, earlier, found, unroll=4)
        done = []
        for n in range(4):
            one = found[n]
            for m in range(n):
                one = one - lower[base + n, base + m : base + m + 1, :] * done[m]
            done.append(one)
            inverse[base + n, :width, :] = one


def pieces_kernel(
    q, k, mixed_v, taps_v, same, cols, rows, inv, within,
    u_out, w_out, qm_out, trans_out, prefix, map_out,
):
    row, column = positions(DK)
    values = [
        silu(convolved(mixed_v[:, of_head(p, DV)], taps_v[:, of_head(p, DV)], same))
        for p in range(PAIR)
    ]
    start = jnp.concatenate([jnp.zeros((DK, DV), F32), jnp.where(row == column, 1.0, 0.0)], 1)
    carried = [start] * PAIR
    for c in range(q.shape[0] // C):
        for p in range(PAIR):
            s, of, of_v = Scalars(cols, rows, p, c), of_head(p, DK), of_head(p, DV)
            key = k[s.at, of]
            value = values[p][c * C : (c + 1) * C]
            solved = dot3c(inv[c, p], jnp.concatenate([value, s.lead * key], 1))
            w = solved[:, DV:]
            u_out[s.at, of_v] = solved[:, :DV]
            w_out[s.at, of] = w
            qm_out[s.at, of] = s.lead * q[s.at, of] - dot3c(within[c, p] * s.beta_row, w)
            both = dot3c(s.close * s.beta * key, solved, TN)
            trans = jnp.where(row == column, s.last, 0.0) - both[:, DV:]
            trans_out[c, p] = trans
            prefix[c, p] = carried[p]
            if c == 0:
                carried[p] = jnp.concatenate([both[:, :DV], trans], 1)
            else:
                new = dot3c(trans, carried[p])
                carried[p] = jnp.concatenate([new[:, :DV] + both[:, :DV], new[:, DV:]], 1)
    for p in range(PAIR):
        map_out[p] = carried[p]


def locals_kernel(u, qm, cols, rows, within, prefix, out, query_map):
    for c in range(u.shape[0] // C):
        for p in range(PAIR):
            s, of, of_v = Scalars(cols, rows, p, c), of_head(p, DK), of_head(p, DV)
            mixed = dot3c(within[c, p] * s.beta_row, u[s.at, of_v])
            if c == 0:
                out[s.at, of_v] = mixed
                query_map[s.at, of] = qm[s.at, of]
            else:
                read = dot3c(qm[s.at, of], prefix[c, p])
                out[s.at, of_v] = mixed + read[:, :DV]
                query_map[s.at, of] = read[:, DV:]


def outputs_kernel(s_in, local, query_map, gate, head_gain, out, gated):
    for p in range(PAIR):
        of, of_v = of_head(p, DK), of_head(p, DV)
        one = local[:, of_v] + dot3c(query_map[:, of], s_in[p])
        out[:, of_v] = one
        scale = lax.rsqrt(total(one * one, 1) * (1.0 / DV) + NORM_EPS)
        gated[:, of_v] = one * scale * head_gain[...] * silu(gate[:, of_v])


def adjoint_piece_kernel(qm, out, gate, head_gain, d_gated, trans, d_out, d_gate, d_gain, direct):
    for p in range(PAIR):
        of_v = of_head(p, DV)
        one, gates, grad = out[:, of_v], gate[:, of_v], d_gated[:, of_v]
        opened = jax.nn.sigmoid(gates)
        scale = lax.rsqrt(total(one * one, 1) * (1.0 / DV) + NORM_EPS)
        scaled = one * scale
        d_scaled = grad * (gates * opened)
        d_gain[p, 0:1] = total(d_scaled * scaled, 0)
        d_gate[:, of_v] = grad * scaled * head_gain[...] * (opened * (1.0 + gates * (1.0 - opened)))
        d_scaled = d_scaled * head_gain[...]
        d_out[:, of_v] = scale * (d_scaled - scaled * (total(d_scaled * scaled, 1) * (1.0 / DV)))
    carried = [None] * PAIR
    for c in reversed(range(qm.shape[0] // C)):
        for p in range(PAIR):
            at = pl.ds(c * C, C)
            here = dot3(qm[at, of_head(p, DK)], d_out[at, of_head(p, DV)], TN)
            if carried[p] is not None:
                here = here + dot3(trans[c, p], carried[p], TN)
            carried[p] = here
    for p in range(PAIR):
        direct[p] = carried[p]


def adjoint_kernel(
    z_in, s_in, q, k, u, w, cols, rows, inv, lower, within, prefix, d_out,
    dq, dk, dv, dcols, drows,
):
    z = [z_in[p] for p in range(PAIR)]
    entered = [split(s_in[p]) for p in range(PAIR)]
    row, column = positions()
    for c in reversed(range(q.shape[0] // C)):
        for p in range(PAIR):
            s, of, of_v = Scalars(cols, rows, p, c), of_head(p, DK), of_head(p, DV)
            key, query = k[s.at, of], q[s.at, of]
            if c == 0:
                state, state_ = s_in[p], entered[p]
            else:
                maps = prefix[c, p]
                state = maps[:, :DV] + dot_halves(*split(maps[:, DV:]), *entered[p])
                state_ = split(state)
            left = u[s.at, of_v] - dot_halves(*split(w[s.at, of]), *state_)
            left_, z_, grad_ = split(left), split(z[p]), split(d_out[s.at, of_v])
            ratios = s.ratios()
            d_left = dot_halves(*split(within[c, p] * s.beta_row), *grad_, TN)
            d_left = d_left + dot_halves(*split(s.close * s.beta * key), *z_)
            e = dot3(inv[c, p], d_left, TN)
            dv[s.at, of_v] = e
            both_ = [jnp.concatenate(pair, 0) for pair in zip(grad_, split(e))]
            back = dot_halves(*both_, *state_, NT)
            d_mix = dot_halves(*both_, *left_, NT)
            d_within = jnp.where(row >= column, d_mix[:C], 0.0)
            d_lower = jnp.where(row > column, -d_mix[C:], 0.0)
            d_close = dot_halves(*left_, *z_, NT)
            d_last = jnp.sum(z[p] * state)
            asks = jnp.concatenate([s.lead * query, -s.lead * key], 0)
            z[p] = s.last * z[p] + dot_halves(*split(asks), *both_, TN)
            scale = ratios * s.beta_row
            pair = jnp.concatenate([d_within * scale, d_lower * scale], 0)
            pair_, key_, query_ = split(pair), split(key), split(query)
            forth = dot_halves(*pair_, *key_)
            lines = [jnp.concatenate(one, 0) for one in zip(query_, key_)]
            dq[s.at, of] = s.lead * back[:C] + forth[:C]
            dk[s.at, of] = (
                s.close * s.beta * d_close
                - s.lead * back[C:]
                + forth[C:]
                + dot_halves(*pair_, *lines, TN)
            )
            share = d_within * within[c, p] + d_lower * lower[c, p]
            drows[p, 0:1, s.at] = total(share, 0)
            dcols[p, s.at, 0:1] = total(share * s.beta_row, 1)
            dcols[p, s.at, 1:2] = total(key * d_close, 1)
            dcols[p, s.at, 2:3] = total(back[:C] * query - back[C:] * key, 1)
            dcols[p, s.at, 3:4] = jnp.full((C, 1), d_last, F32)


def scalars_back_kernel(rows, drows, dcols, out):
    tokens = rows.shape[2]
    from_, to = positions(tokens)
    together = from_ // C == to // C
    reach, alike = (together & (from_ >= to)).astype(BF16), together.astype(BF16)
    place = lax.broadcasted_iota(jnp.int32, (1, tokens), 1)
    d_cums, ends = [], []
    for h in range(H):
        given, cols = rows[h], dcols[h].T
        beta, lead, close = (given[n : n + 1] for n in (BETA, LEAD, CLOSE))
        share = drows[h, 0:1, :]
        out[H + h : H + h + 1, :] = share + close * cols[1:2]
        closing = close * beta * cols[1:2]
        d_cums.append(cols[0:1] - beta * share + lead * cols[2:3] - closing)
        ends.append(closing + jnp.where(place % C == C - 1, lead * cols[3:4], 0.0))
    found = 0.0
    for part, mask in ((jnp.concatenate(d_cums, 0), reach), (jnp.concatenate(ends, 0), alike)):
        high, rest = split(part)
        middle, low = split(part - high.astype(F32))
        found = found + (one_pass(high, mask) + (one_pass(middle, mask) + one_pass(low, mask)))
    out[:H, :] = found


def front_back_kernel(
    mixed_q, mixed_k, mixed_v, taps_q, taps_k, taps_v, same, dq, dk, dv,
    d_mixed_qk, d_mixed_v, d_rim_q, d_rim_k, d_rim_v, d_taps_q, d_taps_k, d_taps_v,
):
    for p in range(PAIR):
        of, of_v = of_head(p, DK), of_head(p, DV)
        for mixed, taps, grad, d_mixed, d_rim, d_taps, factor in (
            (mixed_q, taps_q, dq, d_mixed_qk.at[0], d_rim_q, d_taps_q, DK ** (-0.5)),
            (mixed_k, taps_k, dk, d_mixed_qk.at[1], d_rim_k, d_taps_k, 1.0),
        ):
            act = silu(convolved(mixed[:, of], taps[:, of], same))
            scale = unit(act)
            d_unit = grad[:, of] * factor
            d_act = scale * (d_unit - act * (scale * scale * total(d_unit * act, 1)))
            convolved_back(
                d_act, mixed[:, of], taps[:, of], same,
                d_mixed.at[:, of], d_rim.at[:, of], d_taps.at[:, of],
            )
        convolved_back(
            dv[:, of_v], mixed_v[:, of_v], taps_v[:, of_v], same,
            d_mixed_v.at[:, of_v], d_rim_v.at[:, of_v], d_taps_v.at[:, of_v],
        )


def states_kernel(maps, out):
    state = jnp.zeros((DK, DV), F32)
    for piece in range(maps.shape[0]):
        out[piece] = state
        if piece < maps.shape[0] - 1:
            held = maps[piece]
            state = dot3(held[:, DV:], state) + held[:, :DV]


def adjoints_kernel(maps, direct, out):
    z = jnp.zeros((DK, DV), F32)
    for piece in reversed(range(maps.shape[0])):
        out[piece] = z
        if piece:
            z = dot3(maps[piece][:, DV:], z, TN) + direct[piece]


def whole_call(kernel, args, out_shape, name):
    return call(kernel, (1,), [fixed(a) for a in args], fixed(out_shape), out_shape, name, 4)(*args)


def heads_exchanged(parts):
    return lax.all_to_all(parts, SEQ, 0, 0)


def compose(earlier, later):
    first = jnp.einsum("hij,hjk->hik", later[0], earlier[0], precision=lax.Precision.HIGHEST)
    second = jnp.einsum("hij,hjk->hik", later[0], earlier[1], precision=lax.Precision.HIGHEST)
    return (first, second + later[1])


def entering(part, reverse):
    count, place = lax.axis_size(SEQ), lax.axis_index(SEQ)
    ahead = count - 1 - place if reverse else place
    gathered = jax.tree.map(lambda a: lax.all_gather(a, SEQ), part)
    state = (jnp.broadcast_to(jnp.eye(DK, dtype=F32), part[0].shape), jnp.zeros_like(part[1]))

    def one(step, state):
        source = count - 1 - step if reverse else step
        here = jax.tree.map(lambda a: lax.dynamic_index_in_dim(a, source, 0, False), gathered)
        return compose(state, here)

    return lax.fori_loop(0, ahead, one, state)[1]


BOTH, CROSS, HALF, DOUBLE, SPREAD, COLLECT, OTHER, SUM = range(8)


class Reduction:
    def __init__(self, clock, bits, place, first, way, both):
        self.clock, self.bits, self.at, self.place, self.way = clock, bits, 0, place, way
        self.first = min(first, len(bits) - 1)
        steps = [n for n in range(len(bits)) if n != self.first]
        beyond = [(HALF, n) for n in steps] + [(DOUBLE, n) for n in reversed(steps)]
        if way == 1 and len(bits) == 3:
            beyond = [(SPREAD, 0), (COLLECT, 0)]
        beyond = [(HALF, self.first)] + beyond + [(OTHER, self.first)]
        across = [(BOTH, 0)] if both else [(CROSS, 1), (CROSS, 0)]
        self.plan = across + ([(SUM, 0)] if way == 2 else beyond)

    def grads(self, x, dy, tile, name, us):
        place, shard = self.place, x.shape[1] // 4
        order = [(place & 2 ^ far) | core for core in range(2) for far in (0, 2)]
        bit, half = 0 if self.way == 2 else self.bits[self.first], shard // 2
        starts = jnp.stack([n * shard + (bit ^ part) * half for n in order for part in range(2)])
        (self.sent,) = self.clock.run(lambda x: weight_grad(x, dy, starts, 1, tile, name, us), x)

    def start_near(self):
        self.come = lax.psum_scatter(
            self.clock.gate(self.sent), FSDP, scatter_dimension=0, tiled=True,
            axis_index_groups=couples(),
        )

    def wait_near(self):
        self.clock.wait(self.come)
        shard = self.come.shape[0] // 2
        self.own, self.give = self.come[:shard], self.come[shard:]

    def start(self):
        kind, step = self.plan[self.at]
        half = self.own.shape[0] // 2
        if kind == BOTH:
            parts = [self.give[half:], self.give[:half]]
            self.come = [self.clock.send(part, FSDP, 2) for part in parts]
        elif kind == CROSS:
            part = self.give[half:] if step else self.give[:half]
            self.come = [self.clock.send(part, FSDP, 2)]
        elif kind == HALF:
            self.come = [self.clock.send(self.give, SEQ, 1 << step)]
        elif kind == SPREAD:
            z, size = self.bits[1] | (self.bits[2] << 1), self.own.shape[0] // 4
            self.come = [
                self.clock.send(rows_of(self.own, (z ^ d) * size, size), SEQ, 2 * d)
                for d in (1, 2, 3)
            ]
        elif kind == COLLECT:
            self.come = [self.clock.send(self.own, SEQ, 2 * d) for d in (1, 2, 3)]
        elif kind == SUM:
            own, give = self.clock.gate(self.own), self.clock.gate(self.give)
            self.come = list(lax.psum((own, give), SEQ))
        else:
            self.come = [self.clock.send(self.own, SEQ, 1 << step)]

    def wait(self):
        (kind, step), come = self.plan[self.at], self.come
        self.clock.wait(*come)
        self.at += 1
        if kind == BOTH:
            half = self.own.shape[0] // 2
            self.give, self.own = self.own[half:] + come[0], self.own[:half] + come[1]
        elif kind == CROSS and step:
            self.second = self.own[self.own.shape[0] // 2 :] + come[0]
        elif kind == CROSS:
            self.own, self.give = self.own[: self.own.shape[0] // 2] + come[0], self.second
        elif kind == HALF and self.plan[self.at][0] == HALF:
            whole, bit = self.own + come[0], self.bits[self.plan[self.at][1]]
            half = whole.shape[0] // 2
            self.own = rows_of(whole, bit * half, half)
            self.give = rows_of(whole, (1 - bit) * half, half)
        elif kind == HALF:
            self.own = self.own + come[0]
        elif kind == SPREAD:
            z, size = self.bits[1] | (self.bits[2] << 1), self.own.shape[0] // 4
            self.own = rows_of(self.own, z * size, size) + (come[0] + (come[1] + come[2]))
        elif kind == COLLECT:
            pairs = [self.joined(1, self.own, come[0]), self.joined(1, come[1], come[2])]
            self.own = self.joined(2, *pairs)
        elif kind == DOUBLE:
            self.own = self.joined(step, self.own, come[0])
        elif kind == OTHER:
            self.whole = self.joined(step, self.own, come[0])
        else:
            self.whole = jnp.concatenate(come, 0)

    def joined(self, step, own, come):
        bit = self.bits[step]
        first, second = jnp.where(bit == 0, own, come), jnp.where(bit == 0, come, own)
        return jnp.concatenate([first, second], 0)

    def finish(self):
        self.clock = Free()
        while self.at < len(self.plan):
            self.start()
            self.wait()


def reduced(*parts):
    return jnp.concatenate([r.whole for r in parts], 1)


def on_device(
    residual_in, doc_starts, out_grad, norm_gain, qkv_weight, gate_weight, decay_beta_weight,
    conv_weight, decay_log, decay_bias, beta_bias, head_gain, out_weight, mlp_gain, up_weight,
    down_weight,
):
    place, piece = lax.axis_index(FSDP), lax.axis_index(SEQ)
    pieces = lax.axis_size(SEQ)
    bits = [(piece >> s) & 1 for s in range(pieces.bit_length() - 1)]
    rows, starts, cotangent = residual_in[0], doc_starts[0], out_grad[0]
    tokens = rows.shape[0]
    chunks = tokens // C
    width_k = H * DK
    spread = pieces == H
    clock = Clock()

    counts = jnp.cumsum(starts)
    behind = jnp.flip(jnp.cumsum(jnp.flip(starts))) - starts
    tail_mask = (behind[tokens - CONV + 1 :] == 0).astype(F32)[:, None]
    by_chunk = counts.reshape(chunks, C)
    before = (counts - starts).reshape(chunks, C)[:, :1]
    of_lead = (by_chunk == before).astype(F32)
    of_close = (by_chunk == by_chunk[:, -1:]).astype(F32)
    extended = jnp.concatenate([jnp.zeros((CONV,), jnp.int32), counts])
    same = jnp.stack(
        [(counts == extended[CONV - s : CONV - s + tokens]).astype(F32) for s in range(CONV)], 1
    )
    same = jnp.pad(same, ((0, 0), (0, 8 - CONV)))

    w_qkv, w_gate, w_out, w_up, w_down = (
        Whole(clock, a) for a in (qkv_weight, gate_weight, out_weight, up_weight, down_weight)
    )
    q, k, v, gate, out, up_a, up_b, down = (
        Piece(clock, *given, bits, place)
        for given in (
            (w_qkv, 0, width_k, 0), (w_qkv, width_k, width_k, 0), (w_qkv, 2 * width_k, H * DV, 1),
            (w_gate, 0, H * DV, 0), (w_out, 0, D, 1), (w_up, 0, FF, 0), (w_up, FF, FF, 1),
            (w_down, 0, D, 0),
        )
    )
    small = [norm_gain, decay_beta_weight, conv_weight, decay_log, decay_bias, beta_bias, head_gain, mlp_gain]
    sizes = [a.size for a in small]
    packed = jnp.concatenate([a.reshape(-1) for a in small])

    steps = (H // PAIR,)
    k_spec, v_spec, mixed_k, mixed_v = (
        heads_block(r, w) for r in (tokens, tokens + RIM) for w in (DK, DV)
    )
    taps_q, taps_k = heads_block(CONV, DK), heads_block(CONV, DK, H // PAIR)
    taps_v = heads_block(CONV, DV, H // PAIR)
    cols_spec, rows_spec = per_heads(tokens, 8), per_heads(8, tokens)
    same_spec, gain_spec = fixed(same), fixed(shape(1, DV))
    square_spec, trans_spec, map_spec = (
        per_chunk_heads(chunks, *dims) for dims in ((C, C), (DK, DK), (DK, DV + DK))
    )
    state_spec = per_heads(DK, DV)
    square, state_shape = shape(chunks, H, C, C), shape(H, DK, DV)
    ks, vs = shape(tokens, H * DK), shape(tokens, H * DV)

    for whole in (w_qkv, w_gate, w_out, w_up, w_down):
        whole.near.start()
    come = [clock.send(packed, FSDP, r) for r in range(1, 4)]
    q.far.start()
    clock.wait(*come)
    rim = passed_along(clock.gate(rows[tokens - CONV + 1 :] * tail_mask), SEQ, 1)
    k.far.start()
    clock.wait(rim)

    held = jnp.stack([packed] + come)[jnp.arange(4) ^ place]
    parts, offset = [], 0
    for a, size in zip(small, sizes):
        parts.append(held[:, offset : offset + size].reshape((4,) + a.shape))
        offset += size
    full_norm, full_decay_beta = parts[0].reshape(-1), parts[1].reshape(D, 2 * H)
    taps = jnp.transpose(parts[2], (1, 0, 2)).reshape(CONV, -1)
    decay = [parts[i].reshape(-1) for i in (3, 4, 5)]
    full_head_gain, full_mlp_gain = parts[6].reshape(1, -1), parts[7].reshape(-1)
    normed, norm_pull = jax.vjp(rms_norm, rows, full_norm)
    rim_rows = jnp.pad(rim, ((RIM - CONV + 1, 0), (0, 0)))
    extended_normed = jnp.concatenate([rms_norm(rim_rows, full_norm), normed], 0)
    projected = jnp.dot(normed, full_decay_beta, precision=lax.Precision.HIGHEST)
    (log_decay, beta), scalars_pull = jax.vjp(scalars_of, projected, *decay)
    ahead = jnp.tril(jnp.ones((C, C), F32))
    cum = jnp.einsum(
        "tj,cjh->cth", ahead, log_decay.reshape(chunks, C, H), precision=lax.Precision.HIGHEST
    )
    lead = jnp.exp(cum) * of_lead[:, :, None]
    close = jnp.exp(cum[:, -1:] - cum) * of_close[:, :, None]
    count_cols = jnp.broadcast_to(counts.astype(F32)[:, None], (tokens, H))
    flat = [a.reshape(tokens, H) for a in (cum, beta, lead, close)] + [count_cols]
    rows_in = jnp.stack([a.T for a in flat], 1)
    rows_in = jnp.concatenate([rows_in, jnp.zeros((H, 3, tokens), F32)], 1)
    cols_in = jnp.transpose(rows_in, (0, 2, 1))
    clock.wait(extended_normed, rows_in, cols_in, taps, same)
    clock.wait(*[p.own for p in (q, k, v, gate, out, up_a, up_b, down)])

    def mixed_of(p, name, us):
        weight = p.weight()
        return clock.run(lambda x: block_product(x, weight, 512, name, us), extended_normed)

    q.far.wait()
    q.side.start()
    q.last_a.start()
    v.far.start()
    q.last_a.wait()
    k.far.wait()
    k.side.start()
    k.last_a.start()
    gate.far.start()
    q.side.wait()
    q.last_b.start()
    k.last_a.wait()
    q.last_b.wait()
    w_qkv.near.wait()
    rows_q = mixed_of(q, "q", 8)
    k.side.wait()
    k.last_b.start()
    k.last_b.wait()
    rows_k = mixed_of(k, "k", 8)
    v.far.wait()
    v.side.start()
    v.last_a.start()
    out.far.start()
    queries, key_rows, lower, within, mix = clock.run(
        call(
            keys_kernel, steps,
            [mixed_k, mixed_k, taps_q, taps_k, same_spec, cols_spec, rows_spec],
            [k_spec, k_spec] + [square_spec] * 3, [ks] * 2 + [square] * 3, "keys", 16,
        ),
        rows_q, rows_k, taps, taps, same, cols_in, rows_in,
    )
    v.last_a.wait()
    gate.far.wait()
    gate.side.start()
    gate.last_a.start()
    up_a.far.start()
    lanes = jnp.transpose(mix.reshape(chunks * H, C, C), (1, 2, 0))
    lanes_shape = shape(C, C, chunks * H)
    inverse = clock.run(
        call(inverse_kernel, (1,), [fixed(lanes)], fixed(lanes), lanes_shape, "inverse", 7), lanes
    )
    inverse = jnp.transpose(inverse, (2, 0, 1)).reshape(chunks, H, C, C)
    v.side.wait()
    v.last_b.start()
    gate.last_a.wait()
    v.last_b.wait()
    rows_v = mixed_of(v, "v", 13)
    gate.side.wait()
    gate.last_b.start()
    out.far.wait()
    out.side.start()
    out.last_a.start()
    solved_values, solved_keys, query_map, trans, prefix, map_ = clock.run(
        call(
            pieces_kernel, steps,
            [k_spec, k_spec, mixed_v, taps_v, same_spec, cols_spec, rows_spec, square_spec, square_spec],
            [v_spec, k_spec, k_spec, trans_spec, map_spec, per_heads(DK, DV + DK)],
            [vs, ks, ks, shape(chunks, H, DK, DK), shape(chunks, H, DK, DV + DK), shape(H, DK, DV + DK)],
            "pieces", 30,
        ),
        queries, key_rows, rows_v, taps, same, cols_in, rows_in, inverse, within,
    )
    up_a.far.wait()
    maps = heads_exchanged(clock.gate(map_)) if spread else map_
    up_a.side.start()
    up_a.last_a.start()
    up_b.far.start()
    local_outputs, read_map = clock.run(
        call(
            locals_kernel, steps,
            [v_spec, k_spec, cols_spec, rows_spec, square_spec, map_spec], [v_spec, k_spec], [vs, ks],
            "locals", 12,
        ),
        solved_values, query_map, cols_in, rows_in, within, prefix,
    )
    gate.last_b.wait()
    w_gate.near.wait()
    gate.pack(1024, 8)
    gate_rows = clock.run(lambda x: product(x, gate.packed, 512, "gate", 11), normed)
    out.last_a.wait()
    out.side.wait()
    out.last_b.start()
    if spread:
        clock.wait(maps)
        incoming = clock.run(lambda m: whole_call(states_kernel, [m], state_shape, "states"), maps)
        state_in = heads_exchanged(clock.gate(incoming))
    else:
        state_in = entering((map_[:, :, DV:], map_[:, :, :DV]), False)
    up_a.last_a.wait()
    out.last_b.wait()
    w_out.near.wait()
    out.pack(512, 8)
    up_a.side.wait()
    up_a.last_b.start()
    up_b.far.wait()
    up_b.side.start()
    up_b.last_a.start()
    down.far.start()
    up_a.last_b.wait()
    w_up.near.wait()
    up_a.pack(1408, 9)
    clock.wait(state_in)
    head_outputs, gated = clock.run(
        call(
            outputs_kernel, steps,
            [state_spec, v_spec, k_spec, v_spec, gain_spec], [v_spec] * 2, [vs] * 2, "outputs", 10,
        ),
        state_in, local_outputs, read_map, gate_rows, full_head_gain,
    )
    mixer = clock.run(lambda x: product(x, out.packed, 256, "out", 12), gated)
    middle = rows + mixer
    lifted_in, lifted_pull = jax.vjp(rms_norm, middle, full_mlp_gain)
    up_b.last_a.wait()
    down.far.wait()
    up_b.side.wait()
    up_b.last_b.start()
    down.side.start()
    down.last_a.start()
    up_b.last_b.wait()
    up_b.pack(1408, 9)
    a, b, hidden = clock.run(
        lambda x: lifted_product(x, up_a.packed, up_b.packed, 256, 25), lifted_in
    )
    down.last_a.wait()
    down.side.wait()
    down.last_b.start()

    r_down, r_a, r_b, r_out, r_gate, r_v, r_qk = (
        Reduction(clock, bits, place, first, way, both)
        for first, way, both in (
            (0, 0, 0), (1, 0, 0), (1, 0, 0), (0, 2, 0), (0, 2, 0), (0, 1, 1), (0, 1, 1),
        )
    )
    r_down.grads(hidden, cotangent, 256, "d_down", 18)
    down.last_b.wait()
    w_down.near.wait()
    r_down.start_near()
    down.pack(512, 10)
    r_down.wait_near()

    r_down.start()
    d_a, d_b = clock.run(lambda dy: hidden_back(dy, down.packed, a, b, 256, 20), cotangent)
    r_a.grads(lifted_in, d_a, 1408, "d_a", 17)
    r_down.wait()

    r_down.start()
    r_a.start_near()
    d_lifted = clock.run(lambda dy: product_back(dy, up_a.packed, 256, "back_a", 15), d_a)
    r_b.grads(lifted_in, d_b, 1408, "d_b", 17)
    r_down.wait()
    r_a.wait_near()

    r_a.start()
    r_b.start_near()
    r_down.start()
    d_lifted = clock.run(lambda dy: product_back(dy, up_b.packed, 256, "back_b", 15, d_lifted), d_b)
    d_middle, grad_mlp = lifted_pull(d_lifted)
    d_middle = d_middle + cotangent
    d_gated = clock.run(lambda dy: product_back(dy, out.packed, 256, "d_gated", 12), d_middle)
    d_heads, d_gate, d_gain, direct = clock.run(
        call(
            adjoint_piece_kernel, steps,
            [k_spec, v_spec, v_spec, gain_spec, v_spec, trans_spec],
            [v_spec, v_spec, per_heads(8, DV), state_spec],
            [vs, vs, shape(H, 8, DV), state_shape], "adjoint_piece", 14,
        ),
        query_map, head_outputs, gate_rows, full_head_gain, d_gated, trans,
    )
    r_a.wait()
    r_down.wait()
    r_b.wait_near()

    directs = heads_exchanged(clock.gate(direct)) if spread else direct
    r_a.start()
    r_down.start()
    r_out.grads(gated, d_middle, 512, "d_out", 14)
    r_gate.grads(normed, d_gate, 1024, "d_gate", 14)
    clock.wait(directs)
    r_a.wait()
    r_down.wait()
    if spread:
        outgoing = clock.run(
            lambda d: whole_call(adjoints_kernel, [maps, d], state_shape, "adjoints"), directs
        )
        adjoint_in = heads_exchanged(clock.gate(outgoing))
    else:
        adjoint_in = entering((jnp.swapaxes(map_[:, :, DV:], 1, 2), direct), True)
    r_b.start()
    r_out.start_near()
    r_gate.start_near()
    d_normed = clock.run(lambda dy: product_back(dy, gate.packed, 256, "back_gate", 12), d_gate)
    branch = clock.run(lambda x: product(x, down.packed, 256, "down", 14), hidden)
    clock.wait(adjoint_in)
    r_b.wait()
    r_out.wait_near()
    r_gate.wait_near()

    r_b.start()
    r_out.start()
    r_a.start()
    r_down.start()
    d_queries, d_keys, d_values, dcols, drows = clock.run(
        call(
            adjoint_kernel, steps,
            [state_spec, state_spec, k_spec, k_spec, v_spec, k_spec, cols_spec, rows_spec,
             square_spec, square_spec, square_spec, map_spec, v_spec],
            [k_spec, k_spec, v_spec, cols_spec, rows_spec],
            [ks, ks, vs, shape(H, tokens, 8), shape(H, 8, tokens)], "adjoint", 55,
        ),
        adjoint_in, state_in, queries, key_rows, solved_values, solved_keys, cols_in, rows_in,
        inverse, lower, within, prefix, d_heads,
    )
    for r in (r_b, r_out, r_a, r_down):
        r.wait()

    for r in (r_out, r_a, r_down):
        r.start()
    rim_k, rim_v, tap_k, tap_v = (heads_block(r, w) for r in (RIM, CONV) for w in (DK, DV))
    qk_spec = pl.BlockSpec((2, tokens, PAIR * DK), lambda h: (0, 0, h))
    d_qk, d_v, *rest = clock.run(
        call(
            front_back_kernel, steps,
            [mixed_k, mixed_k, mixed_v, taps_q, taps_k, taps_v, same_spec, k_spec, k_spec, v_spec],
            [qk_spec, v_spec, rim_k, rim_k, rim_v, tap_k, tap_k, tap_v],
            [shape(2, tokens, width_k), vs] + [shape(r, H * w) for r in (RIM, CONV) for w in (DK, DK, DV)],
            "front_back", 25,
        ),
        rows_q, rows_k, rows_v, taps, taps, taps, same, d_queries, d_keys, d_values,
    )
    d_rims, grad_conv = jnp.concatenate(rest[:3], 1)[RIM - 8 :], jnp.concatenate(rest[3:], 1)
    for r in (r_out, r_a, r_down):
        r.wait()

    returned = passed_along(clock.gate(d_rims), SEQ, -1)
    clock.wait(returned)
    returned = returned * jnp.pad(tail_mask, ((8 - CONV + 1, 0), (0, 0)))
    more = jnp.stack([returned[:, :width_k], returned[:, width_k : 2 * width_k]])
    d_qk = lax.dynamic_update_slice(d_qk, d_qk[:, tokens - 8 :] + more, (0, tokens - 8, 0))
    last = d_v[tokens - 8 :] + returned[:, 2 * width_k :]
    d_v = lax.dynamic_update_slice(d_v, last, (tokens - 8, 0))

    for r in (r_gate, r_b, r_a):
        r.start()
    r_v.grads(normed, d_v, 1024, "d_v", 13)
    r_qk.grads(normed, d_qk, 1024, "d_qk", 13)
    for r in (r_gate, r_b, r_a):
        r.wait()

    for r in (r_gate, r_b, r_down, r_a):
        r.start()
    r_v.start_near()
    r_qk.start_near()
    d_normed = clock.run(
        lambda dy: block_product_back([(dy, v.weight())], 512, "back_v", 15, d_normed), d_v
    )
    r_v.wait_near()
    for r in (r_gate, r_b, r_down, r_a):
        r.wait()

    for r in (r_v, r_b, r_a, r_down):
        r.start()
    d_normed = clock.run(
        lambda dy: block_product_back(
            [(dy, q.weight()), (dy, k.weight())], 256, "back_qk", 15, d_normed
        ),
        d_qk,
    )
    args = [rows_in, drows, dcols]
    scalars_shape = shape(2 * H, tokens)
    found = clock.run(
        call(
            scalars_back_kernel, (1,), [fixed(a) for a in args], fixed(scalars_shape), scalars_shape,
            "scalars_back", 5,
        ),
        *args,
    )
    r_qk.wait_near()
    r_out.start()
    r_gate.start()
    for r in (r_b, r_a, r_v, r_down):
        r.wait()

    for r in (r_qk, r_v, r_b, r_a):
        r.start()
    d_projected, *grad_decay = scalars_pull((clock.gate(found[:H]).T, found[H:].T))
    grad_decay_beta = dot(normed, d_projected, TN)
    d_normed = d_normed + dot(d_projected, full_decay_beta, NT)
    d_rows, grad_norm = norm_pull(d_normed)
    row_grad, result = d_rows + d_middle, middle + branch
    squares = jnp.stack([jnp.sum(x * x) for x in (rows, mixer, branch, result)])
    small_grads = [
        grad_norm, grad_decay_beta, jnp.transpose(grad_conv.reshape(CONV, 4, -1), (1, 0, 2)),
        *grad_decay, jnp.sum(d_gain[:, 0], 0), grad_mlp, jnp.broadcast_to(squares, (4, 4)),
    ]
    rows4 = jnp.concatenate([x.reshape(4, -1) for x in small_grads], 1)[jnp.arange(4) ^ place]
    small_sum = SmallSum(clock, rows4, bits)
    clock.wait(rows4)
    r_v.wait()
    r_v.start()
    for r in (r_b, r_a, r_qk, r_v):
        r.wait()

    for group in ((r_qk, r_v, small_sum), (r_qk, r_v, small_sum), (r_qk, r_b, small_sum), (r_qk, r_b, small_sum)):
        for r in group:
            r.start()
        for r in group:
            r.wait()
    small_sum.start()
    small_sum.wait()
    r_out.wait()
    r_gate.wait()
    for r in (r_down, r_a, r_b, r_out, r_gate, r_v, r_qk):
        r.finish()
    summed = small_sum.finish()

    out_small, offset = [], 0
    for x, size in zip(small, sizes):
        out_small.append(summed[offset : offset + size].reshape(x.shape))
        offset += size
    count = pieces * lax.axis_size(FSDP) * tokens * D
    grad_norm, grad_decay_beta, grad_conv, grad_log, grad_bias, grad_beta, grad_head, grad_mlp = out_small
    return (
        result[None], row_grad[None], grad_norm, reduced(r_qk, r_v), reduced(r_gate),
        grad_decay_beta, grad_conv, grad_log, grad_bias, grad_beta, grad_head, reduced(r_out),
        grad_mlp, reduced(r_a, r_b), reduced(r_down), jnp.sqrt(summed[offset:] / count),
    )


def solution(mesh):
    split_tokens = P(FSDP, SEQ, None)
    lines = P(FSDP, None)
    return jax.shard_map(
        on_device,
        mesh=mesh,
        in_specs=(
            split_tokens, P(FSDP, SEQ), split_tokens, P(FSDP), lines, lines, lines,
            P(None, FSDP), P(FSDP), P(FSDP), P(FSDP), P(FSDP), lines, P(FSDP), lines, lines,
        ),
        out_specs=(
            split_tokens, split_tokens, P(FSDP), lines, lines, lines, P(None, FSDP),
            P(FSDP), P(FSDP), P(FSDP), P(FSDP), lines, P(FSDP), lines, lines, P(),
        ),
        check_vma=False,
    )
```

```python
from functools import partial

import jax
import jax.numpy as jnp
from jax import lax
from jax.experimental import pallas as pl
from jax.experimental.pallas import tpu as pltpu
from jax.sharding import PartitionSpec as P

D = 1024
H = 8
DK = 128
DV = 256
FF = 2816
CONV = 4
C = 64
FSDP, SEQ = "fsdp", "seq"
RIM = 16
PAIR = 2

NORM_EPS = 1e-05
UNIT_EPS = 1e-06
F32 = jnp.float32
BF16 = jnp.bfloat16
VMEM_BYTES = 56 * 1024 * 1024

NN = (((1,), (0,)), ((), ()))
NT = (((1,), (1,)), ((), ()))
TN = (((0,), (0,)), ((), ()))


def swapped(block, axis, distance):
    return lax.ppermute(block, axis, [(i, i ^ distance) for i in range(lax.axis_size(axis))])


def passed_along(block, axis, distance):
    devices = range(lax.axis_size(axis))
    route = [(i - distance, i) for i in devices if i - distance in devices]
    return lax.ppermute(block, axis, route)


def rows_of(block, start, size):
    return lax.dynamic_slice_in_dim(block, start, size, 0)


class Free:
    def gate(self, value):
        return value

    def wait(self, *done):
        pass

    def send(self, block, axis, distance):
        return swapped(block, axis, distance)


class Clock:
    def __init__(self):
        self.token = jnp.zeros((8, 128), F32)

    def wait(self, *done):
        self.token = lax.optimization_barrier((self.token,) + done)[0]

    def gate(self, value):
        return lax.optimization_barrier((value, self.token))[0]

    def send(self, block, axis, distance):
        return swapped(self.gate(block), axis, distance)

    def run(self, kernel, first, *rest):
        found = kernel(self.gate(first), *rest)
        self.wait(found[0] if isinstance(found, (list, tuple)) else found)
        return found


class Transfer:
    def __init__(self, clock, source, move):
        self.clock, self.source, self.move = clock, source, move

    def start(self):
        self.come = self.move(self.clock.gate(self.source()))

    def wait(self):
        self.clock.wait(self.come)


def swap(axis, distance):
    return lambda block: swapped(block, axis, distance)


def couples():
    return [[i, i + 1] for i in range(0, lax.axis_size(FSDP), 2)]


class Whole:
    def __init__(self, clock, shard):
        self.shard = shard
        self.near = Transfer(
            clock,
            lambda: shard,
            lambda a: lax.all_gather(a, FSDP, axis=0, tiled=True, axis_index_groups=couples()),
        )


class Piece:
    def __init__(self, clock, whole, column, width, step, bits, place):
        self.clock, self.whole, self.column, self.width = clock, whole, column, width
        self.bit, self.place = bits[min(step, len(bits) - 1)], place
        half = whole.shard.shape[0] // 2
        self.own = lax.dynamic_slice(whole.shard, (self.bit * half, column), (half, width))
        step = min(step, len(bits) - 1)
        self.far = Transfer(clock, lambda: self.own, swap(FSDP, 2))
        self.side = Transfer(clock, lambda: self.far.come, swap(SEQ, 1 << step))
        self.last_a = Transfer(clock, lambda: self.far.come, swap(FSDP, 1))
        self.last_b = Transfer(clock, lambda: self.side.come, swap(FSDP, 1))

    def weight(self):
        shard, place = self.whole.shard.shape[0], self.place
        half = shard // 2
        blocks = [self.whole.near.come] + [
            t.come for t in (self.far, self.side, self.last_a, self.last_b)
        ]
        starts = [(place & 2) * shard] + [
            (place ^ r) * shard + (self.bit ^ part) * half for r in (2, 3) for part in range(2)
        ]
        return Weight(blocks, [self.column] + [0] * 4, self.width, [1] * 5, jnp.stack(starts))

    def pack(self, tile, us):
        weight = self.weight()
        weight.blocks[0] = self.clock.gate(weight.blocks[0])
        self.packed = packed_weight(weight, tile, us)
        self.clock.wait(*self.packed)


class SmallSum:
    def __init__(self, clock, rows4, bits):
        self.clock, self.rows, self.at, self.count = clock, rows4, 0, len(bits)

    def start(self):
        block = (self.rows[1::2], self.rows[1:])[self.at] if self.at < 2 else self.rows
        axis, distance = (FSDP, 1 << self.at) if self.at < 2 else (SEQ, 1 << (self.at - 2))
        self.come = self.clock.send(block, axis, distance)

    def wait(self):
        self.clock.wait(self.come)
        kept = (self.rows[0::2], self.rows[:1])[self.at] if self.at < 2 else self.rows
        self.rows, self.at = kept + self.come, self.at + 1

    def finish(self):
        self.clock = Free()
        while self.at < 2 + self.count:
            self.start()
            self.wait()
        return self.rows[0]


def split(x):
    high = x.astype(BF16)
    return high, (x - high.astype(F32)).astype(BF16)


def one_pass(left, right, dims=NN):
    return lax.dot_general(left, right, dims, preferred_element_type=F32)


def dot_halves(lh, ll, rh, rl, dims=NN):
    return one_pass(lh, rh, dims) + (one_pass(lh, rl, dims) + one_pass(ll, rh, dims))


def stacked(ref, x):
    rows = x.shape[0]
    ref[:rows], ref[rows:] = split(x)


def dot_stacked(left, high, low, dims=NN):
    rows = left.shape[0] // 2
    top = one_pass(left[...], high, dims)
    return top[:rows] + (top[rows:] + one_pass(left[:rows], low, dims))


def dot3(left, right, dims=NN):
    return dot_halves(*split(left), *split(right), dims)


def dot3c(left, right, dims=NN):
    (one,), (two,) = dims[0]
    lh, ll = split(left)
    rh, rl = split(right)
    left = jnp.concatenate([lh, lh, ll], one)
    right = jnp.concatenate([rh, rl, rh], two)
    return lax.dot_general(left, right, dims, preferred_element_type=F32)


def dot(left, right, dims=NN):
    return lax.dot_general(
        left, right, dims, precision=lax.Precision.HIGH, preferred_element_type=F32
    )


def shape(*dims):
    return jax.ShapeDtypeStruct(dims, F32)


def cost(us):
    return pl.CostEstimate(flops=int(us), bytes_accessed=1024, transcendentals=0)


def call(kernel, grid, in_specs, out_specs, out_shape, name, us, scratch=(), prefetch=0):
    return pl.pallas_call(
        kernel,
        grid_spec=pltpu.PrefetchScalarGridSpec(
            num_scalar_prefetch=prefetch,
            grid=grid,
            in_specs=in_specs,
            out_specs=out_specs,
            scratch_shapes=scratch,
        ),
        out_shape=out_shape,
        name=name,
        compiler_params=pltpu.CompilerParams(
            vmem_limit_bytes=VMEM_BYTES, dimension_semantics=("arbitrary",) * len(grid)
        ),
        cost_estimate=cost(us),
    )


def fixed(array):
    return pl.BlockSpec(array.shape, lambda j, *_: (0,) * len(array.shape))


class Weight:
    def __init__(self, blocks, columns, width, parts, starts):
        self.blocks, self.columns, self.width = blocks, columns, width
        self.parts, self.starts = parts, starts

    def specs(self, tile):
        return [
            pl.BlockSpec((block.shape[0], tile), lambda j, *_, shift=column // tile: (0, j + shift))
            for block, column in zip(self.blocks, self.columns)
        ]


def place_weight(starts, refs, parts, high, low, columns):
    n = 0
    for ref, count in zip(refs, parts):
        size = ref.shape[0] // count
        for part in range(count):
            at = pl.ds(pl.multiple_of(starts[n], 16), size)
            high[at, columns], low[at, columns] = split(ref[part * size : (part + 1) * size])
            n += 1


def block_product(x, weight, tile, name, us):
    tokens, depth = x.shape
    width = weight.width
    count = len(weight.blocks)

    def kernel(starts, x_ref, *refs):
        blocks, refs = refs[:count], refs[count:]
        out, xs, wh, wl = refs

        @pl.when(pl.program_id(0) == 0)
        def _():
            stacked(xs, x_ref[...])

        place_weight(starts, blocks, weight.parts, wh, wl, slice(None))
        out[...] = dot_stacked(xs, wh[...], wl[...])

    tiled = pl.BlockSpec((tokens, tile), lambda j, *_: (0, j))
    return call(
        kernel,
        (width // tile,),
        [fixed(x)] + weight.specs(tile),
        tiled,
        shape(tokens, width),
        name,
        us,
        [pltpu.VMEM((2 * tokens, depth), BF16)] + [pltpu.VMEM((depth, tile), BF16)] * 2,
        prefetch=1,
    )(weight.starts, x, *weight.blocks)


def block_product_back(parts, tile, name, us, add=None):
    tokens, width = parts[0][0].shape[-2:]
    depth = 2 * parts[0][1].blocks[0].shape[0]
    count = len(parts[0][1].blocks)
    planes = parts[0][0].ndim == 3
    steps = width // tile
    n = len(parts)

    def kernel(starts, *refs):
        dys, refs = refs[: 1 if planes else n], refs[1 if planes else n :]
        blocks, refs = refs[: n * count], refs[n * count :]
        if add is not None:
            add_ref, refs = refs[0], refs[1:]
        out, wh, wl = refs
        for p in range(n):
            columns = slice(p * tile, (p + 1) * tile)
            refs_ = blocks[p * count : (p + 1) * count]
            place_weight(starts, refs_, parts[p][1].parts, wh, wl, columns)
        dy = jnp.concatenate([dys[0][p] for p in range(n)], 1) if planes else dys[0][...]
        found = dot_halves(*split(dy), wh[...], wl[...], NT)

        @pl.when(pl.program_id(0) == 0)
        def _():
            out[...] = found if add is None else found + add_ref[...]

        @pl.when(pl.program_id(0) > 0)
        def _():
            out[...] += found

    tiled = pl.BlockSpec((tokens, tile), lambda j, *_: (0, j))
    whole = pl.BlockSpec((tokens, depth), lambda j, *_: (0, 0))
    specs, arrays = [tiled], [parts[0][0]]
    if planes:
        specs = [pl.BlockSpec((n, tokens, tile), lambda j, *_: (0, 0, j))]
    for _, weight in parts:
        specs += weight.specs(tile)
        arrays += weight.blocks
    if add is not None:
        specs, arrays = specs + [whole], arrays + [add]
    return call(
        kernel, (steps,), specs, whole, shape(tokens, depth), name, us,
        [pltpu.VMEM((depth, n * tile), BF16)] * 2, prefetch=1,
    )(parts[0][1].starts, *arrays)


def packed_weight(weight, tile, us):
    depth, width = 2 * weight.blocks[0].shape[0], weight.width

    def kernel(starts, *refs):
        place_weight(starts, refs[:-2], weight.parts, *refs[-2:], slice(None))

    return call(
        kernel,
        (width // tile,),
        weight.specs(tile),
        [pl.BlockSpec((depth, tile), lambda j, *_: (0, j))] * 2,
        [jax.ShapeDtypeStruct((depth, width), BF16)] * 2,
        "packed",
        us,
        prefetch=1,
    )(weight.starts, *weight.blocks)


def product(x, weight, tile, name, us):
    tokens, depth = x.shape
    width = weight[0].shape[1]

    def kernel(x_ref, high, low, out, xs):
        @pl.when(pl.program_id(0) == 0)
        def _():
            stacked(xs, x_ref[...])

        out[...] = dot_stacked(xs, high[...], low[...])

    tiled = pl.BlockSpec((tokens, tile), lambda j: (0, j))
    weights = pl.BlockSpec((depth, tile), lambda j: (0, j))
    return call(
        kernel, (width // tile,), [fixed(x), weights, weights], tiled, shape(tokens, width),
        name, us, [pltpu.VMEM((2 * tokens, depth), BF16)],
    )(x, *weight)


def lifted_product(x, weight_a, weight_b, tile, us):
    tokens, depth = x.shape

    def kernel(x_ref, ah, al, bh, bl, a_out, b_out, hidden, xs):
        @pl.when(pl.program_id(0) == 0)
        def _():
            stacked(xs, x_ref[...])

        a = dot_stacked(xs, ah[...], al[...])
        b = dot_stacked(xs, bh[...], bl[...])
        a_out[...] = a
        b_out[...] = b
        hidden[...] = a * jax.nn.sigmoid(a) * b

    tiled = pl.BlockSpec((tokens, tile), lambda j: (0, j))
    weights = pl.BlockSpec((depth, tile), lambda j: (0, j))
    return call(
        kernel, (FF // tile,), [fixed(x)] + [weights] * 4, [tiled] * 3, [shape(tokens, FF)] * 3,
        "lifted", us, [pltpu.VMEM((2 * tokens, depth), BF16)],
    )(x, *weight_a, *weight_b)


def product_back(dy, weight, tile, name, us, add=None):
    tokens, width = dy.shape
    depth = weight[0].shape[0]

    def kernel(dy_ref, high, low, *refs):
        out, ds = refs[-2:]

        @pl.when(pl.program_id(0) == 0)
        def _():
            stacked(ds, dy_ref[...])

        found = dot_stacked(ds, high[...], low[...], NT)
        out[...] = found if add is None else found + refs[0][...]

    tiled = pl.BlockSpec((tokens, tile), lambda j: (0, j))
    weights = pl.BlockSpec((tile, width), lambda j: (j, 0))
    more = [] if add is None else [add]
    return call(
        kernel, (depth // tile,), [fixed(dy), weights, weights] + [tiled] * len(more), tiled,
        shape(tokens, depth), name, us, [pltpu.VMEM((2 * tokens, width), BF16)],
    )(dy, *weight, *more)


def hidden_back(dy, weight, a, b, tile, us):
    tokens, width = dy.shape

    def kernel(dy_ref, high, low, a_ref, b_ref, d_a, d_b, ds):
        @pl.when(pl.program_id(0) == 0)
        def _():
            stacked(ds, dy_ref[...])

        found = dot_stacked(ds, high[...], low[...], NT)
        opened = jax.nn.sigmoid(a_ref[...])
        d_a[...] = found * b_ref[...] * opened * (1.0 + a_ref[...] * (1.0 - opened))
        d_b[...] = found * a_ref[...] * opened

    tiled = pl.BlockSpec((tokens, tile), lambda j: (0, j))
    weights = pl.BlockSpec((tile, width), lambda j: (j, 0))
    return call(
        kernel, (FF // tile,), [fixed(dy), weights, weights, tiled, tiled], [tiled] * 2,
        [shape(tokens, FF)] * 2, "hidden_back", us, [pltpu.VMEM((2 * tokens, width), BF16)],
    )(dy, *weight, a, b)


def weight_grad(x, dy, halves, groups, tile, name, us, add=None):
    tokens, depth = x.shape
    half, count = depth // 8, halves.shape[0]
    planes = dy.ndim == 3
    width = dy.shape[0] * dy.shape[2] if planes else dy.shape[1]
    size = count * half // groups

    def kernel(halves, x_ref, dy_ref, *refs):
        adds, refs = (refs[:groups], refs[groups:]) if add is not None else ((), refs)
        outs, (xt, xs) = refs[:groups], refs[groups:]

        @pl.when(pl.program_id(0) == 0)
        def _():
            xt[...] = x_ref[...].T
            for n in range(count):
                high, low = split(xt[pl.ds(pl.multiple_of(halves[n], 16), half), :])
                xs[n * half : (n + 1) * half] = high
                xs[(count + n) * half : (count + n + 1) * half] = low

        found = dot_stacked(xs, *split(dy_ref[0] if planes else dy_ref[...]))
        for n in range(groups):
            block = found[n * size : (n + 1) * size]
            outs[n][...] = block + adds[n][...] if adds else block

    tiled = pl.BlockSpec((size, tile), lambda j, *_: (0, j))
    added = [pl.BlockSpec((size, tile), lambda j, *_, n=n: (n, j)) for n in range(groups)]
    of_dy = pl.BlockSpec((tokens, tile), lambda j, *_: (0, j))
    if planes:
        each = dy.shape[2] // tile
        of_dy = pl.BlockSpec((1, tokens, tile), lambda j, *_: (j // each, 0, j % each))
    more = [add] * groups if add is not None else []
    return call(
        kernel,
        (width // tile,),
        [fixed(x), of_dy] + added[: len(more)],
        [tiled] * groups,
        [shape(size, width)] * groups,
        name,
        us,
        [pltpu.VMEM((depth, tokens), F32), pltpu.VMEM((2 * count * half, tokens), BF16)],
        prefetch=1,
    )(halves, x, dy, *more)


def rms_norm(rows, gain):
    return rows * lax.rsqrt(jnp.mean(rows * rows, axis=-1, keepdims=True) + NORM_EPS) * gain


def scalars_of(decay_beta, decay_log, decay_bias, beta_bias):
    log_decay = -jnp.exp(decay_log) * jax.nn.softplus(decay_beta[:, :H] + decay_bias)
    return log_decay, jax.nn.sigmoid(decay_beta[:, H:] + beta_bias)


def total(x, axis):
    return jnp.sum(x, axis, keepdims=True)


def unit(x):
    return lax.rsqrt(total(x * x, 1) + UNIT_EPS)


def convolved(mixed, taps, same):
    tokens = mixed.shape[0] - RIM
    found = taps[0:1] * mixed[RIM:]
    for s in range(1, CONV):
        found = found + taps[s : s + 1] * (mixed[RIM - s : RIM - s + tokens] * same[:, s : s + 1])
    return found


def convolved_back(d_act, mixed, taps, same, d_mixed, d_rim, d_taps):
    tokens, width = d_act.shape
    before = convolved(mixed, taps, same)
    gate = jax.nn.sigmoid(before)
    d_before = d_act * gate * (1.0 + before * (1.0 - gate))
    empty = jnp.zeros((RIM, width), F32)
    found = jnp.concatenate([empty, taps[0:1] * d_before], 0)
    d_taps[0:1] = total(d_before * mixed[RIM:], 0)
    for s in range(1, CONV):
        reached = d_before * same[:, s : s + 1]
        padded = jnp.concatenate([empty, reached, empty], 0)
        found = found + taps[s : s + 1] * padded[s : s + RIM + tokens]
        d_taps[s : s + 1] = total(reached * mixed[RIM - s : RIM - s + tokens], 0)
    d_mixed[...] = found[RIM:]
    d_rim[...] = found[:RIM]


def silu(x):
    return x * jax.nn.sigmoid(x)


def heads_block(rows, width, shift=0):
    return pl.BlockSpec((rows, PAIR * width), lambda h, *_: (0, h + shift))


def per_heads(*dims):
    return pl.BlockSpec((PAIR,) + dims, lambda h, *_: (h,) + (0,) * len(dims))


def per_chunk_heads(chunks, *dims):
    return pl.BlockSpec((chunks, PAIR) + dims, lambda h, *_: (0, h) + (0,) * len(dims))


def positions(size=C):
    row = lax.broadcasted_iota(jnp.int32, (size, size), 0)
    column = lax.broadcasted_iota(jnp.int32, (size, size), 1)
    return row, column


CUM, BETA, LEAD, CLOSE, COUNT = 0, 1, 2, 3, 4


class Scalars:
    def __init__(self, cols, rows, p, c):
        at = pl.ds(c * C, C)
        self.at = at
        block, lines = cols[p, at, :], rows[p, :, at]
        self.cum, self.beta = block[:, CUM : CUM + 1], block[:, BETA : BETA + 1]
        self.lead, self.close = block[:, LEAD : LEAD + 1], block[:, CLOSE : CLOSE + 1]
        self.count = block[:, COUNT : COUNT + 1]
        self.last = block[C - 1 : C, LEAD : LEAD + 1]
        self.cum_row, self.beta_row = lines[CUM : CUM + 1], lines[BETA : BETA + 1]
        self.count_row = lines[COUNT : COUNT + 1]

    def ratios(self):
        row, column = positions()
        near = (self.count == self.count_row) & (row >= column)
        return jnp.where(near, jnp.exp(jnp.minimum(self.cum - self.cum_row, 0.0)), 0.0)


def of_head(p, width):
    return slice(p * width, (p + 1) * width)


def keys_kernel(mixed_q, mixed_k, taps_q, taps_k, same, cols, rows, q, k, lower, within, lower_mix):
    row, column = positions()
    for p in range(PAIR):
        of = of_head(p, DK)
        act = silu(convolved(mixed_q[:, of], taps_q[:, of], same))
        q[:, of] = act * unit(act) * DK ** (-0.5)
        act = silu(convolved(mixed_k[:, of], taps_k[:, of], same))
        k[:, of] = act * unit(act)
    for c in range(q.shape[0] // C):
        for p in range(PAIR):
            s, of = Scalars(cols, rows, p, c), of_head(p, DK)
            key = k[s.at, of]
            dots = dot3c(jnp.concatenate([key, q[s.at, of]], 0), key, NT)
            ratios = s.ratios()
            below = jnp.where(row > column, ratios, 0.0) * dots[:C]
            lower[c, p] = below
            lower_mix[c, p] = below * s.beta_row
            within[c, p] = ratios * dots[C:]


def inverse_kernel(lower, inverse):
    lanes = lower.shape[2]
    inverse[...] = jnp.zeros(inverse.shape, F32)
    for base in range(0, C, 4):
        width = (base + 4 + 7) // 8 * 8
        place = lax.broadcasted_iota(jnp.int32, (width, lanes), 0)
        found = tuple(jnp.where(place == base + n, 1.0, 0.0).astype(F32) for n in range(4))

        def earlier(j, found):
            known = inverse[j, :width, :]
            return tuple(f - lower[base + n, pl.ds(j, 1), :] * known for n, f in enumerate(found))

        if base:
            found = lax.fori_loop(0, base, earlier, found, unroll=4)
        done = []
        for n in range(4):
            one = found[n]
            for m in range(n):
                one = one - lower[base + n, base + m : base + m + 1, :] * done[m]
            done.append(one)
            inverse[base + n, :width, :] = one


def pieces_kernel(
    q, k, mixed_v, taps_v, same, cols, rows, inv, within,
    u_out, w_out, qm_out, trans_out, prefix, map_out,
):
    row, column = positions(DK)
    values = [
        silu(convolved(mixed_v[:, of_head(p, DV)], taps_v[:, of_head(p, DV)], same))
        for p in range(PAIR)
    ]
    start = jnp.concatenate([jnp.zeros((DK, DV), F32), jnp.where(row == column, 1.0, 0.0)], 1)
    carried = [start] * PAIR
    for c in range(q.shape[0] // C):
        for p in range(PAIR):
            s, of, of_v = Scalars(cols, rows, p, c), of_head(p, DK), of_head(p, DV)
            key = k[s.at, of]
            value = values[p][c * C : (c + 1) * C]
            solved = dot3c(inv[c, p], jnp.concatenate([value, s.lead * key], 1))
            w = solved[:, DV:]
            u_out[s.at, of_v] = solved[:, :DV]
            w_out[s.at, of] = w
            qm_out[s.at, of] = s.lead * q[s.at, of] - dot3c(within[c, p] * s.beta_row, w)
            both = dot3c(s.close * s.beta * key, solved, TN)
            trans = jnp.where(row == column, s.last, 0.0) - both[:, DV:]
            trans_out[c, p] = trans
            prefix[c, p] = carried[p]
            if c == 0:
                carried[p] = jnp.concatenate([both[:, :DV], trans], 1)
            else:
                new = dot3c(trans, carried[p])
                carried[p] = jnp.concatenate([new[:, :DV] + both[:, :DV], new[:, DV:]], 1)
    for p in range(PAIR):
        map_out[p] = carried[p]


def locals_kernel(u, qm, cols, rows, within, prefix, out, query_map):
    for c in range(u.shape[0] // C):
        for p in range(PAIR):
            s, of, of_v = Scalars(cols, rows, p, c), of_head(p, DK), of_head(p, DV)
            mixed = dot3c(within[c, p] * s.beta_row, u[s.at, of_v])
            if c == 0:
                out[s.at, of_v] = mixed
                query_map[s.at, of] = qm[s.at, of]
            else:
                read = dot3c(qm[s.at, of], prefix[c, p])
                out[s.at, of_v] = mixed + read[:, :DV]
                query_map[s.at, of] = read[:, DV:]


def outputs_kernel(s_in, local, query_map, gate, head_gain, out, gated):
    for p in range(PAIR):
        of, of_v = of_head(p, DK), of_head(p, DV)
        one = local[:, of_v] + dot3c(query_map[:, of], s_in[p])
        out[:, of_v] = one
        scale = lax.rsqrt(total(one * one, 1) * (1.0 / DV) + NORM_EPS)
        gated[:, of_v] = one * scale * head_gain[...] * silu(gate[:, of_v])


def adjoint_piece_kernel(qm, out, gate, head_gain, d_gated, trans, d_out, d_gate, d_gain, direct):
    for p in range(PAIR):
        of_v = of_head(p, DV)
        one, gates, grad = out[:, of_v], gate[:, of_v], d_gated[:, of_v]
        opened = jax.nn.sigmoid(gates)
        scale = lax.rsqrt(total(one * one, 1) * (1.0 / DV) + NORM_EPS)
        scaled = one * scale
        d_scaled = grad * (gates * opened)
        d_gain[p, 0:1] = total(d_scaled * scaled, 0)
        d_gate[:, of_v] = grad * scaled * head_gain[...] * (opened * (1.0 + gates * (1.0 - opened)))
        d_scaled = d_scaled * head_gain[...]
        d_out[:, of_v] = scale * (d_scaled - scaled * (total(d_scaled * scaled, 1) * (1.0 / DV)))
    carried = [None] * PAIR
    for c in reversed(range(qm.shape[0] // C)):
        for p in range(PAIR):
            at = pl.ds(c * C, C)
            here = dot3(qm[at, of_head(p, DK)], d_out[at, of_head(p, DV)], TN)
            if carried[p] is not None:
                here = here + dot3(trans[c, p], carried[p], TN)
            carried[p] = here
    for p in range(PAIR):
        direct[p] = carried[p]


def adjoint_kernel(
    z_in, s_in, q, k, u, w, cols, rows, inv, lower, within, prefix, d_out,
    dq, dk, dv, dcols, drows,
):
    z = [z_in[p] for p in range(PAIR)]
    entered = [split(s_in[p]) for p in range(PAIR)]
    row, column = positions()
    for c in reversed(range(q.shape[0] // C)):
        for p in range(PAIR):
            s, of, of_v = Scalars(cols, rows, p, c), of_head(p, DK), of_head(p, DV)
            key, query = k[s.at, of], q[s.at, of]
            if c == 0:
                state, state_ = s_in[p], entered[p]
            else:
                maps = prefix[c, p]
                state = maps[:, :DV] + dot_halves(*split(maps[:, DV:]), *entered[p])
                state_ = split(state)
            left = u[s.at, of_v] - dot_halves(*split(w[s.at, of]), *state_)
            left_, z_, grad_ = split(left), split(z[p]), split(d_out[s.at, of_v])
            ratios = s.ratios()
            d_left = dot_halves(*split(within[c, p] * s.beta_row), *grad_, TN)
            d_left = d_left + dot_halves(*split(s.close * s.beta * key), *z_)
            e = dot3(inv[c, p], d_left, TN)
            dv[s.at, of_v] = e
            both_ = [jnp.concatenate(pair, 0) for pair in zip(grad_, split(e))]
            back = dot_halves(*both_, *state_, NT)
            d_mix = dot_halves(*both_, *left_, NT)
            d_within = jnp.where(row >= column, d_mix[:C], 0.0)
            d_lower = jnp.where(row > column, -d_mix[C:], 0.0)
            d_close = dot_halves(*left_, *z_, NT)
            d_last = jnp.sum(z[p] * state)
            asks = jnp.concatenate([s.lead * query, -s.lead * key], 0)
            z[p] = s.last * z[p] + dot_halves(*split(asks), *both_, TN)
            scale = ratios * s.beta_row
            pair = jnp.concatenate([d_within * scale, d_lower * scale], 0)
            pair_, key_, query_ = split(pair), split(key), split(query)
            forth = dot_halves(*pair_, *key_)
            lines = [jnp.concatenate(one, 0) for one in zip(query_, key_)]
            dq[s.at, of] = s.lead * back[:C] + forth[:C]
            dk[s.at, of] = (
                s.close * s.beta * d_close
                - s.lead * back[C:]
                + forth[C:]
                + dot_halves(*pair_, *lines, TN)
            )
            share = d_within * within[c, p] + d_lower * lower[c, p]
            drows[p, 0:1, s.at] = total(share, 0)
            dcols[p, s.at, 0:1] = total(share * s.beta_row, 1)
            dcols[p, s.at, 1:2] = total(key * d_close, 1)
            dcols[p, s.at, 2:3] = total(back[:C] * query - back[C:] * key, 1)
            dcols[p, s.at, 3:4] = jnp.full((C, 1), d_last, F32)


def scalars_back_kernel(rows, drows, dcols, out):
    tokens = rows.shape[2]
    from_, to = positions(tokens)
    together = from_ // C == to // C
    reach, alike = (together & (from_ >= to)).astype(BF16), together.astype(BF16)
    place = lax.broadcasted_iota(jnp.int32, (1, tokens), 1)
    d_cums, ends = [], []
    for h in range(H):
        given, cols = rows[h], dcols[h].T
        beta, lead, close = (given[n : n + 1] for n in (BETA, LEAD, CLOSE))
        share = drows[h, 0:1, :]
        out[H + h : H + h + 1, :] = share + close * cols[1:2]
        closing = close * beta * cols[1:2]
        d_cums.append(cols[0:1] - beta * share + lead * cols[2:3] - closing)
        ends.append(closing + jnp.where(place % C == C - 1, lead * cols[3:4], 0.0))
    found = 0.0
    for part, mask in ((jnp.concatenate(d_cums, 0), reach), (jnp.concatenate(ends, 0), alike)):
        high, rest = split(part)
        middle, low = split(part - high.astype(F32))
        found = found + (one_pass(high, mask) + (one_pass(middle, mask) + one_pass(low, mask)))
    out[:H, :] = found


def front_back_kernel(
    mixed_q, mixed_k, mixed_v, taps_q, taps_k, taps_v, same, dq, dk, dv,
    d_mixed_qk, d_mixed_v, d_rim_q, d_rim_k, d_rim_v, d_taps_q, d_taps_k, d_taps_v,
):
    for p in range(PAIR):
        of, of_v = of_head(p, DK), of_head(p, DV)
        for mixed, taps, grad, d_mixed, d_rim, d_taps, factor in (
            (mixed_q, taps_q, dq, d_mixed_qk.at[0], d_rim_q, d_taps_q, DK ** (-0.5)),
            (mixed_k, taps_k, dk, d_mixed_qk.at[1], d_rim_k, d_taps_k, 1.0),
        ):
            act = silu(convolved(mixed[:, of], taps[:, of], same))
            scale = unit(act)
            d_unit = grad[:, of] * factor
            d_act = scale * (d_unit - act * (scale * scale * total(d_unit * act, 1)))
            convolved_back(
                d_act, mixed[:, of], taps[:, of], same,
                d_mixed.at[:, of], d_rim.at[:, of], d_taps.at[:, of],
            )
        convolved_back(
            dv[:, of_v], mixed_v[:, of_v], taps_v[:, of_v], same,
            d_mixed_v.at[:, of_v], d_rim_v.at[:, of_v], d_taps_v.at[:, of_v],
        )


def states_kernel(maps, out):
    state = jnp.zeros((DK, DV), F32)
    for piece in range(maps.shape[0]):
        out[piece] = state
        if piece < maps.shape[0] - 1:
            held = maps[piece]
            state = dot3(held[:, DV:], state) + held[:, :DV]


def adjoints_kernel(maps, direct, out):
    z = jnp.zeros((DK, DV), F32)
    for piece in reversed(range(maps.shape[0])):
        out[piece] = z
        if piece:
            z = dot3(maps[piece][:, DV:], z, TN) + direct[piece]


def whole_call(kernel, args, out_shape, name):
    return call(kernel, (1,), [fixed(a) for a in args], fixed(out_shape), out_shape, name, 4)(*args)


def heads_exchanged(parts):
    return lax.all_to_all(parts, SEQ, 0, 0)


def compose(earlier, later):
    first = jnp.einsum("hij,hjk->hik", later[0], earlier[0], precision=lax.Precision.HIGHEST)
    second = jnp.einsum("hij,hjk->hik", later[0], earlier[1], precision=lax.Precision.HIGHEST)
    return (first, second + later[1])


def entering(part, reverse):
    count, place = lax.axis_size(SEQ), lax.axis_index(SEQ)
    ahead = count - 1 - place if reverse else place
    gathered = jax.tree.map(lambda a: lax.all_gather(a, SEQ), part)
    state = (jnp.broadcast_to(jnp.eye(DK, dtype=F32), part[0].shape), jnp.zeros_like(part[1]))

    def one(step, state):
        source = count - 1 - step if reverse else step
        here = jax.tree.map(lambda a: lax.dynamic_index_in_dim(a, source, 0, False), gathered)
        return compose(state, here)

    return lax.fori_loop(0, ahead, one, state)[1]


BOTH, CROSS, HALF, DOUBLE, SPREAD, COLLECT, OTHER, SUM = range(8)


class Reduction:
    def __init__(self, clock, bits, place, first, way, both):
        self.clock, self.bits, self.at, self.place, self.way = clock, bits, 0, place, way
        self.first = min(first, len(bits) - 1)
        steps = [n for n in range(len(bits)) if n != self.first]
        beyond = [(HALF, n) for n in steps] + [(DOUBLE, n) for n in reversed(steps)]
        if way == 1 and len(bits) == 3:
            beyond = [(SPREAD, 0), (COLLECT, 0)]
        beyond = [(HALF, self.first)] + beyond + [(OTHER, self.first)]
        across = [(BOTH, 0)] if both else [(CROSS, 1), (CROSS, 0)]
        self.plan = across + ([(SUM, 0)] if way == 2 else beyond)

    def grads(self, x, dy, tile, name, us):
        place, shard = self.place, x.shape[1] // 4
        order = [(place & 2 ^ far) | core for core in range(2) for far in (0, 2)]
        bit, half = 0 if self.way == 2 else self.bits[self.first], shard // 2
        starts = jnp.stack([n * shard + (bit ^ part) * half for n in order for part in range(2)])
        (self.sent,) = self.clock.run(lambda x: weight_grad(x, dy, starts, 1, tile, name, us), x)

    def start_near(self):
        self.come = lax.psum_scatter(
            self.clock.gate(self.sent), FSDP, scatter_dimension=0, tiled=True,
            axis_index_groups=couples(),
        )

    def wait_near(self):
        self.clock.wait(self.come)
        shard = self.come.shape[0] // 2
        self.own, self.give = self.come[:shard], self.come[shard:]

    def start(self):
        kind, step = self.plan[self.at]
        half = self.own.shape[0] // 2
        if kind == BOTH:
            parts = [self.give[half:], self.give[:half]]
            self.come = [self.clock.send(part, FSDP, 2) for part in parts]
        elif kind == CROSS:
            part = self.give[half:] if step else self.give[:half]
            self.come = [self.clock.send(part, FSDP, 2)]
        elif kind == HALF:
            self.come = [self.clock.send(self.give, SEQ, 1 << step)]
        elif kind == SPREAD:
            z, size = self.bits[1] | (self.bits[2] << 1), self.own.shape[0] // 4
            self.come = [
                self.clock.send(rows_of(self.own, (z ^ d) * size, size), SEQ, 2 * d)
                for d in (1, 2, 3)
            ]
        elif kind == COLLECT:
            self.come = [self.clock.send(self.own, SEQ, 2 * d) for d in (1, 2, 3)]
        elif kind == SUM:
            own, give = self.clock.gate(self.own), self.clock.gate(self.give)
            self.come = list(lax.psum((own, give), SEQ))
        else:
            self.come = [self.clock.send(self.own, SEQ, 1 << step)]

    def wait(self):
        (kind, step), come = self.plan[self.at], self.come
        self.clock.wait(*come)
        self.at += 1
        if kind == BOTH:
            half = self.own.shape[0] // 2
            self.give, self.own = self.own[half:] + come[0], self.own[:half] + come[1]
        elif kind == CROSS and step:
            self.second = self.own[self.own.shape[0] // 2 :] + come[0]
        elif kind == CROSS:
            self.own, self.give = self.own[: self.own.shape[0] // 2] + come[0], self.second
        elif kind == HALF and self.plan[self.at][0] == HALF:
            whole, bit = self.own + come[0], self.bits[self.plan[self.at][1]]
            half = whole.shape[0] // 2
            self.own = rows_of(whole, bit * half, half)
            self.give = rows_of(whole, (1 - bit) * half, half)
        elif kind == HALF:
            self.own = self.own + come[0]
        elif kind == SPREAD:
            z, size = self.bits[1] | (self.bits[2] << 1), self.own.shape[0] // 4
            self.own = rows_of(self.own, z * size, size) + (come[0] + (come[1] + come[2]))
        elif kind == COLLECT:
            pairs = [self.joined(1, self.own, come[0]), self.joined(1, come[1], come[2])]
            self.own = self.joined(2, *pairs)
        elif kind == DOUBLE:
            self.own = self.joined(step, self.own, come[0])
        elif kind == OTHER:
            self.whole = self.joined(step, self.own, come[0])
        else:
            self.whole = jnp.concatenate(come, 0)

    def joined(self, step, own, come):
        bit = self.bits[step]
        first, second = jnp.where(bit == 0, own, come), jnp.where(bit == 0, come, own)
        return jnp.concatenate([first, second], 0)

    def finish(self):
        self.clock = Free()
        while self.at < len(self.plan):
            self.start()
            self.wait()


def reduced(*parts):
    return jnp.concatenate([r.whole for r in parts], 1)


def on_device(
    residual_in, doc_starts, out_grad, norm_gain, qkv_weight, gate_weight, decay_beta_weight,
    conv_weight, decay_log, decay_bias, beta_bias, head_gain, out_weight, mlp_gain, up_weight,
    down_weight,
):
    place, piece = lax.axis_index(FSDP), lax.axis_index(SEQ)
    pieces = lax.axis_size(SEQ)
    bits = [(piece >> s) & 1 for s in range(pieces.bit_length() - 1)]
    rows, starts, cotangent = residual_in[0], doc_starts[0], out_grad[0]
    tokens = rows.shape[0]
    chunks = tokens // C
    width_k = H * DK
    spread = pieces == H
    clock = Clock()

    counts = jnp.cumsum(starts)
    behind = jnp.flip(jnp.cumsum(jnp.flip(starts))) - starts
    tail_mask = (behind[tokens - CONV + 1 :] == 0).astype(F32)[:, None]
    by_chunk = counts.reshape(chunks, C)
    before = (counts - starts).reshape(chunks, C)[:, :1]
    of_lead = (by_chunk == before).astype(F32)
    of_close = (by_chunk == by_chunk[:, -1:]).astype(F32)
    extended = jnp.concatenate([jnp.zeros((CONV,), jnp.int32), counts])
    same = jnp.stack(
        [(counts == extended[CONV - s : CONV - s + tokens]).astype(F32) for s in range(CONV)], 1
    )
    same = jnp.pad(same, ((0, 0), (0, 8 - CONV)))

    w_qkv, w_gate, w_out, w_up, w_down = (
        Whole(clock, a) for a in (qkv_weight, gate_weight, out_weight, up_weight, down_weight)
    )
    q, k, v, gate, out, up_a, up_b, down = (
        Piece(clock, *given, bits, place)
        for given in (
            (w_qkv, 0, width_k, 0), (w_qkv, width_k, width_k, 0), (w_qkv, 2 * width_k, H * DV, 1),
            (w_gate, 0, H * DV, 0), (w_out, 0, D, 1), (w_up, 0, FF, 0), (w_up, FF, FF, 1),
            (w_down, 0, D, 0),
        )
    )
    small = [norm_gain, decay_beta_weight, conv_weight, decay_log, decay_bias, beta_bias, head_gain, mlp_gain]
    sizes = [a.size for a in small]
    packed = jnp.concatenate([a.reshape(-1) for a in small])

    steps = (H // PAIR,)
    k_spec, v_spec, mixed_k, mixed_v = (
        heads_block(r, w) for r in (tokens, tokens + RIM) for w in (DK, DV)
    )
    taps_q, taps_k = heads_block(CONV, DK), heads_block(CONV, DK, H // PAIR)
    taps_v = heads_block(CONV, DV, H // PAIR)
    cols_spec, rows_spec = per_heads(tokens, 8), per_heads(8, tokens)
    same_spec, gain_spec = fixed(same), fixed(shape(1, DV))
    square_spec, trans_spec, map_spec = (
        per_chunk_heads(chunks, *dims) for dims in ((C, C), (DK, DK), (DK, DV + DK))
    )
    state_spec = per_heads(DK, DV)
    square, state_shape = shape(chunks, H, C, C), shape(H, DK, DV)
    ks, vs = shape(tokens, H * DK), shape(tokens, H * DV)

    for whole in (w_qkv, w_gate, w_out, w_up, w_down):
        whole.near.start()
    come = [clock.send(packed, FSDP, r) for r in range(1, 4)]
    q.far.start()
    clock.wait(*come)
    rim = passed_along(clock.gate(rows[tokens - CONV + 1 :] * tail_mask), SEQ, 1)
    k.far.start()
    clock.wait(rim)

    held = jnp.stack([packed] + come)[jnp.arange(4) ^ place]
    parts, offset = [], 0
    for a, size in zip(small, sizes):
        parts.append(held[:, offset : offset + size].reshape((4,) + a.shape))
        offset += size
    full_norm, full_decay_beta = parts[0].reshape(-1), parts[1].reshape(D, 2 * H)
    taps = jnp.transpose(parts[2], (1, 0, 2)).reshape(CONV, -1)
    decay = [parts[i].reshape(-1) for i in (3, 4, 5)]
    full_head_gain, full_mlp_gain = parts[6].reshape(1, -1), parts[7].reshape(-1)
    normed, norm_pull = jax.vjp(rms_norm, rows, full_norm)
    rim_rows = jnp.pad(rim, ((RIM - CONV + 1, 0), (0, 0)))
    extended_normed = jnp.concatenate([rms_norm(rim_rows, full_norm), normed], 0)
    projected = jnp.dot(normed, full_decay_beta, precision=lax.Precision.HIGHEST)
    (log_decay, beta), scalars_pull = jax.vjp(scalars_of, projected, *decay)
    ahead = jnp.tril(jnp.ones((C, C), F32))
    cum = jnp.einsum(
        "tj,cjh->cth", ahead, log_decay.reshape(chunks, C, H), precision=lax.Precision.HIGHEST
    )
    lead = jnp.exp(cum) * of_lead[:, :, None]
    close = jnp.exp(cum[:, -1:] - cum) * of_close[:, :, None]
    count_cols = jnp.broadcast_to(counts.astype(F32)[:, None], (tokens, H))
    flat = [a.reshape(tokens, H) for a in (cum, beta, lead, close)] + [count_cols]
    rows_in = jnp.stack([a.T for a in flat], 1)
    rows_in = jnp.concatenate([rows_in, jnp.zeros((H, 3, tokens), F32)], 1)
    cols_in = jnp.transpose(rows_in, (0, 2, 1))
    clock.wait(extended_normed, rows_in, cols_in, taps, same)
    clock.wait(*[p.own for p in (q, k, v, gate, out, up_a, up_b, down)])

    def mixed_of(p, name, us):
        weight = p.weight()
        return clock.run(lambda x: block_product(x, weight, 512, name, us), extended_normed)

    q.far.wait()
    q.side.start()
    q.last_a.start()
    v.far.start()
    q.last_a.wait()
    k.far.wait()
    k.side.start()
    k.last_a.start()
    gate.far.start()
    q.side.wait()
    q.last_b.start()
    k.last_a.wait()
    q.last_b.wait()
    w_qkv.near.wait()
    rows_q = mixed_of(q, "q", 8)
    k.side.wait()
    k.last_b.start()
    k.last_b.wait()
    rows_k = mixed_of(k, "k", 8)
    v.far.wait()
    v.side.start()
    v.last_a.start()
    out.far.start()
    queries, key_rows, lower, within, mix = clock.run(
        call(
            keys_kernel, steps,
            [mixed_k, mixed_k, taps_q, taps_k, same_spec, cols_spec, rows_spec],
            [k_spec, k_spec] + [square_spec] * 3, [ks] * 2 + [square] * 3, "keys", 16,
        ),
        rows_q, rows_k, taps, taps, same, cols_in, rows_in,
    )
    v.last_a.wait()
    gate.far.wait()
    gate.side.start()
    gate.last_a.start()
    up_a.far.start()
    lanes = jnp.transpose(mix.reshape(chunks * H, C, C), (1, 2, 0))
    lanes_shape = shape(C, C, chunks * H)
    inverse = clock.run(
        call(inverse_kernel, (1,), [fixed(lanes)], fixed(lanes), lanes_shape, "inverse", 7), lanes
    )
    inverse = jnp.transpose(inverse, (2, 0, 1)).reshape(chunks, H, C, C)
    v.side.wait()
    v.last_b.start()
    gate.last_a.wait()
    v.last_b.wait()
    rows_v = mixed_of(v, "v", 13)
    gate.side.wait()
    gate.last_b.start()
    solved_values, solved_keys, query_map, trans, prefix, map_ = clock.run(
        call(
            pieces_kernel, steps,
            [k_spec, k_spec, mixed_v, taps_v, same_spec, cols_spec, rows_spec, square_spec, square_spec],
            [v_spec, k_spec, k_spec, trans_spec, map_spec, per_heads(DK, DV + DK)],
            [vs, ks, ks, shape(chunks, H, DK, DK), shape(chunks, H, DK, DV + DK), shape(H, DK, DV + DK)],
            "pieces", 30,
        ),
        queries, key_rows, rows_v, taps, same, cols_in, rows_in, inverse, within,
    )
    out.far.wait()
    up_a.far.wait()
    maps = heads_exchanged(clock.gate(map_)) if spread else map_
    out.side.start()
    out.last_a.start()
    up_a.side.start()
    up_a.last_a.start()
    up_b.far.start()
    local_outputs, read_map = clock.run(
        call(
            locals_kernel, steps,
            [v_spec, k_spec, cols_spec, rows_spec, square_spec, map_spec], [v_spec, k_spec], [vs, ks],
            "locals", 12,
        ),
        solved_values, query_map, cols_in, rows_in, within, prefix,
    )
    gate.last_b.wait()
    w_gate.near.wait()
    gate.pack(1024, 8)
    gate_rows = clock.run(lambda x: product(x, gate.packed, 512, "gate", 11), normed)
    out.last_a.wait()
    out.side.wait()
    out.last_b.start()
    if spread:
        clock.wait(maps)
        incoming = clock.run(lambda m: whole_call(states_kernel, [m], state_shape, "states"), maps)
        state_in = heads_exchanged(clock.gate(incoming))
    else:
        state_in = entering((map_[:, :, DV:], map_[:, :, :DV]), False)
    up_a.last_a.wait()
    out.last_b.wait()
    w_out.near.wait()
    out.pack(512, 8)
    up_a.side.wait()
    up_a.last_b.start()
    up_b.far.wait()
    up_b.side.start()
    up_b.last_a.start()
    down.far.start()
    up_a.last_b.wait()
    w_up.near.wait()
    up_a.pack(1408, 9)
    clock.wait(state_in)
    head_outputs, gated = clock.run(
        call(
            outputs_kernel, steps,
            [state_spec, v_spec, k_spec, v_spec, gain_spec], [v_spec] * 2, [vs] * 2, "outputs", 10,
        ),
        state_in, local_outputs, read_map, gate_rows, full_head_gain,
    )
    mixer = clock.run(lambda x: product(x, out.packed, 256, "out", 12), gated)
    middle = rows + mixer
    lifted_in, lifted_pull = jax.vjp(rms_norm, middle, full_mlp_gain)
    up_b.last_a.wait()
    down.far.wait()
    up_b.side.wait()
    up_b.last_b.start()
    down.side.start()
    down.last_a.start()
    up_b.last_b.wait()
    up_b.pack(1408, 9)
    a, b, hidden = clock.run(
        lambda x: lifted_product(x, up_a.packed, up_b.packed, 256, 25), lifted_in
    )
    down.last_a.wait()
    down.side.wait()
    down.last_b.start()

    r_down, r_a, r_b, r_out, r_gate, r_v, r_qk = (
        Reduction(clock, bits, place, first, way, both)
        for first, way, both in (
            (0, 0, 0), (1, 0, 0), (1, 0, 0), (0, 2, 0), (0, 2, 0), (0, 1, 1), (0, 1, 1),
        )
    )
    r_down.grads(hidden, cotangent, 256, "d_down", 18)
    down.last_b.wait()
    w_down.near.wait()
    r_down.start_near()
    down.pack(512, 10)
    r_down.wait_near()

    r_down.start()
    d_a, d_b = clock.run(lambda dy: hidden_back(dy, down.packed, a, b, 256, 20), cotangent)
    r_a.grads(lifted_in, d_a, 1408, "d_a", 17)
    r_down.wait()

    r_down.start()
    r_a.start_near()
    d_lifted = clock.run(lambda dy: product_back(dy, up_a.packed, 256, "back_a", 15), d_a)
    r_b.grads(lifted_in, d_b, 1408, "d_b", 17)
    r_down.wait()
    r_a.wait_near()

    r_a.start()
    r_b.start_near()
    r_down.start()
    d_lifted = clock.run(lambda dy: product_back(dy, up_b.packed, 256, "back_b", 15, d_lifted), d_b)
    d_middle, grad_mlp = lifted_pull(d_lifted)
    d_middle = d_middle + cotangent
    d_gated = clock.run(lambda dy: product_back(dy, out.packed, 256, "d_gated", 12), d_middle)
    d_heads, d_gate, d_gain, direct = clock.run(
        call(
            adjoint_piece_kernel, steps,
            [k_spec, v_spec, v_spec, gain_spec, v_spec, trans_spec],
            [v_spec, v_spec, per_heads(8, DV), state_spec],
            [vs, vs, shape(H, 8, DV), state_shape], "adjoint_piece", 14,
        ),
        query_map, head_outputs, gate_rows, full_head_gain, d_gated, trans,
    )
    r_a.wait()
    r_down.wait()
    r_b.wait_near()

    directs = heads_exchanged(clock.gate(direct)) if spread else direct
    r_a.start()
    r_down.start()
    r_out.grads(gated, d_middle, 512, "d_out", 14)
    r_gate.grads(normed, d_gate, 1024, "d_gate", 14)
    clock.wait(directs)
    r_a.wait()
    r_down.wait()
    if spread:
        outgoing = clock.run(
            lambda d: whole_call(adjoints_kernel, [maps, d], state_shape, "adjoints"), directs
        )
        adjoint_in = heads_exchanged(clock.gate(outgoing))
    else:
        adjoint_in = entering((jnp.swapaxes(map_[:, :, DV:], 1, 2), direct), True)
    r_b.start()
    r_out.start_near()
    r_gate.start_near()
    d_normed = clock.run(lambda dy: product_back(dy, gate.packed, 256, "back_gate", 12), d_gate)
    branch = clock.run(lambda x: product(x, down.packed, 256, "down", 14), hidden)
    clock.wait(adjoint_in)
    r_b.wait()
    r_out.wait_near()
    r_gate.wait_near()

    r_b.start()
    r_out.start()
    r_a.start()
    r_down.start()
    d_queries, d_keys, d_values, dcols, drows = clock.run(
        call(
            adjoint_kernel, steps,
            [state_spec, state_spec, k_spec, k_spec, v_spec, k_spec, cols_spec, rows_spec,
             square_spec, square_spec, square_spec, map_spec, v_spec],
            [k_spec, k_spec, v_spec, cols_spec, rows_spec],
            [ks, ks, vs, shape(H, tokens, 8), shape(H, 8, tokens)], "adjoint", 55,
        ),
        adjoint_in, state_in, queries, key_rows, solved_values, solved_keys, cols_in, rows_in,
        inverse, lower, within, prefix, d_heads,
    )
    for r in (r_b, r_out, r_a, r_down):
        r.wait()

    for r in (r_out, r_a, r_down):
        r.start()
    rim_k, rim_v, tap_k, tap_v = (heads_block(r, w) for r in (RIM, CONV) for w in (DK, DV))
    qk_spec = pl.BlockSpec((2, tokens, PAIR * DK), lambda h: (0, 0, h))
    d_qk, d_v, *rest = clock.run(
        call(
            front_back_kernel, steps,
            [mixed_k, mixed_k, mixed_v, taps_q, taps_k, taps_v, same_spec, k_spec, k_spec, v_spec],
            [qk_spec, v_spec, rim_k, rim_k, rim_v, tap_k, tap_k, tap_v],
            [shape(2, tokens, width_k), vs] + [shape(r, H * w) for r in (RIM, CONV) for w in (DK, DK, DV)],
            "front_back", 25,
        ),
        rows_q, rows_k, rows_v, taps, taps, taps, same, d_queries, d_keys, d_values,
    )
    d_rims, grad_conv = jnp.concatenate(rest[:3], 1)[RIM - 8 :], jnp.concatenate(rest[3:], 1)
    for r in (r_out, r_a, r_down):
        r.wait()

    returned = passed_along(clock.gate(d_rims), SEQ, -1)
    clock.wait(returned)
    returned = returned * jnp.pad(tail_mask, ((8 - CONV + 1, 0), (0, 0)))
    more = jnp.stack([returned[:, :width_k], returned[:, width_k : 2 * width_k]])
    d_qk = lax.dynamic_update_slice(d_qk, d_qk[:, tokens - 8 :] + more, (0, tokens - 8, 0))
    last = d_v[tokens - 8 :] + returned[:, 2 * width_k :]
    d_v = lax.dynamic_update_slice(d_v, last, (tokens - 8, 0))

    for r in (r_gate, r_b, r_a):
        r.start()
    r_v.grads(normed, d_v, 1024, "d_v", 13)
    r_qk.grads(normed, d_qk, 1024, "d_qk", 13)
    for r in (r_gate, r_b, r_a):
        r.wait()

    for r in (r_gate, r_b, r_down, r_a):
        r.start()
    r_v.start_near()
    r_qk.start_near()
    d_normed = clock.run(
        lambda dy: block_product_back([(dy, v.weight())], 512, "back_v", 15, d_normed), d_v
    )
    r_v.wait_near()
    for r in (r_gate, r_b, r_down, r_a):
        r.wait()

    for r in (r_v, r_b, r_a, r_down, r_out, r_gate):
        r.start()
    d_normed = clock.run(
        lambda dy: block_product_back(
            [(dy, q.weight()), (dy, k.weight())], 256, "back_qk", 15, d_normed
        ),
        d_qk,
    )
    args = [rows_in, drows, dcols]
    scalars_shape = shape(2 * H, tokens)
    found = clock.run(
        call(
            scalars_back_kernel, (1,), [fixed(a) for a in args], fixed(scalars_shape), scalars_shape,
            "scalars_back", 5,
        ),
        *args,
    )
    r_qk.wait_near()
    for r in (r_b, r_a, r_v, r_down):
        r.wait()

    for r in (r_qk, r_v, r_b, r_a):
        r.start()
    d_projected, *grad_decay = scalars_pull((clock.gate(found[:H]).T, found[H:].T))
    grad_decay_beta = dot(normed, d_projected, TN)
    d_normed = d_normed + dot(d_projected, full_decay_beta, NT)
    d_rows, grad_norm = norm_pull(d_normed)
    row_grad, result = d_rows + d_middle, middle + branch
    squares = jnp.stack([jnp.sum(x * x) for x in (rows, mixer, branch, result)])
    small_grads = [
        grad_norm, grad_decay_beta, jnp.transpose(grad_conv.reshape(CONV, 4, -1), (1, 0, 2)),
        *grad_decay, jnp.sum(d_gain[:, 0], 0), grad_mlp, jnp.broadcast_to(squares, (4, 4)),
    ]
    rows4 = jnp.concatenate([x.reshape(4, -1) for x in small_grads], 1)[jnp.arange(4) ^ place]
    small_sum = SmallSum(clock, rows4, bits)
    clock.wait(rows4)
    r_v.wait()
    r_v.start()
    for r in (r_b, r_a, r_qk, r_v):
        r.wait()

    for group in ((r_qk, r_v, small_sum), (r_qk, r_v, small_sum), (r_qk, r_b, small_sum), (r_qk, r_b, small_sum)):
        for r in group:
            r.start()
        for r in group:
            r.wait()
    small_sum.start()
    small_sum.wait()
    r_out.wait()
    r_gate.wait()
    for r in (r_down, r_a, r_b, r_out, r_gate, r_v, r_qk):
        r.finish()
    summed = small_sum.finish()

    out_small, offset = [], 0
    for x, size in zip(small, sizes):
        out_small.append(summed[offset : offset + size].reshape(x.shape))
        offset += size
    count = pieces * lax.axis_size(FSDP) * tokens * D
    grad_norm, grad_decay_beta, grad_conv, grad_log, grad_bias, grad_beta, grad_head, grad_mlp = out_small
    return (
        result[None], row_grad[None], grad_norm, reduced(r_qk, r_v), reduced(r_gate),
        grad_decay_beta, grad_conv, grad_log, grad_bias, grad_beta, grad_head, reduced(r_out),
        grad_mlp, reduced(r_a, r_b), reduced(r_down), jnp.sqrt(summed[offset:] / count),
    )


def solution(mesh):
    split_tokens = P(FSDP, SEQ, None)
    lines = P(FSDP, None)
    return jax.shard_map(
        on_device,
        mesh=mesh,
        in_specs=(
            split_tokens, P(FSDP, SEQ), split_tokens, P(FSDP), lines, lines, lines,
            P(None, FSDP), P(FSDP), P(FSDP), P(FSDP), P(FSDP), lines, P(FSDP), lines, lines,
        ),
        out_specs=(
            split_tokens, split_tokens, P(FSDP), lines, lines, lines, P(None, FSDP),
            P(FSDP), P(FSDP), P(FSDP), P(FSDP), lines, P(FSDP), lines, lines, P(),
        ),
        check_vma=False,
    )
```
